128 devices in a mesh: tm: 32 (over z, y_hi, x), space: 4 (over y_lo, core).
Axes of the slice: x: 4, y: 4 (y_hi: 2, y_lo: 2; y = y_hi * 2 + y_lo), z: 4, core: 2. Of those that a mesh axis runs over, the one named last changes fastest.
Arguments:
- initial_field: float32 [48, 2048], P(None, 'space'), may hold values from -6 to 6
- decay_rates: float32 [48, 2048], P(None, 'space'), may hold values from 0.001 to 1
- source: float32 [48, 2048], P(None, 'space'), may hold values from -5 to 5
- diffusion: float32 [48], replicated, may hold values from 0.02 to 0.5
- saturation: float32 [48], replicated, may hold values from 0.1 to 1
- conversion: float32 [48, 48], replicated, may hold values from 0.01 to 0.5
Outputs:
- coarse_points: float32 [32, 48, 2048], P('tm', None, 'space')
The draws below stay inside these ranges and needn't reach their ends.
All inputs are finite; a program needn't handle non-finite values.
Results may differ from the reference program's by a relative error of at most 0.0003.
Values may be sent and summed in bfloat16 or wider, within the bound.
No kernel may reach another device: no remote copies, remote signals or barrier semaphores. Data moves between devices by JAX's collectives and lax.ppermute only.
A program may use at most 128 MiB of HBM per device.

```python
import math
import jax
import jax.numpy as jnp
from jax import lax

S = 48
COLS = 128
FACTOR = 4
NEWTON = 2
CYCLES = 2
INTERVALS = 32
CELLS = 2048


def shard_levels(key, dims, split, low, high):
    def one(dim, parts):
        steps = jax.random.uniform(jax.random.fold_in(jax.random.fold_in(key, 6), dim), (parts,), jnp.float32, low / len(split), high / len(split))
        return jnp.repeat(jnp.exp(steps), dims[dim] // parts).reshape((-1,) + (1,) * (len(dims) - dim - 1))

    level = one(*split[0])
    for cut in split[1:]:
        level = level * one(*cut)
    return level


def bell_draw(key, dims, deviation, limit, shards=(), kind=jnp.bfloat16):
    result = jax.random.normal(key, dims, jnp.float32) * deviation
    if len(shards) > 0:
        result = shard_levels(key, dims, shards, -0.22, 0.18) * result
    return jnp.clip(result, min=-limit, max=limit).astype(kind)


def setup_inputs(seed: int = 0) -> dict:
    splits = jax.random.split(jax.random.key(seed), 7)
    return {
        "initial_field": bell_draw(splits[0], (S, CELLS), 1.0, 6.0, ((1, 4),), jnp.float32),
        "decay_rates": jnp.clip(jnp.exp(math.log(1.0) - 6.9077552 * jax.random.uniform(splits[1], (S, CELLS), jnp.float32) ** shard_levels(splits[1], (S, CELLS), ((1, 4),), -0.2, 0.2)), 0.001, 1.0),
        "source": bell_draw(splits[2], (S, CELLS), 1.0, 5.0, ((1, 4),), jnp.float32),
        "diffusion": jnp.clip(jnp.exp(jax.random.uniform(splits[3], (S,), jnp.float32, math.log(0.02), math.log(0.5))), 0.02, 0.5),
        "saturation": jnp.clip(jnp.exp(jax.random.uniform(splits[4], (S,), jnp.float32, math.log(0.1), math.log(1.0))), 0.1, 1.0),
        "conversion": jnp.clip(jnp.exp(jax.random.uniform(splits[5], (S, S), jnp.float32, math.log(0.01), math.log(0.5))), 0.01, 0.5),
    }


precise = lax.Precision.HIGHEST


def conversion_parts(conversion):
    species = conversion.shape[0]
    identity = jnp.eye(species, dtype=jnp.float32)
    off_diagonal = conversion * (1.0 - identity)
    return off_diagonal, jnp.sum(off_diagonal, axis=0)


def laplace(padded, columns, cell_count):
    middle = padded[:, columns:columns + cell_count]
    upper_row = padded[:, 0:cell_count]
    lower_row = padded[:, 2 * columns:2 * columns + cell_count]
    left_side = padded[:, columns - 1:columns - 1 + cell_count]
    right_side = padded[:, columns + 1:columns + 1 + cell_count]
    position = jnp.arange(cell_count, dtype=jnp.int32) % columns
    left_side = jnp.where(position[None, :] != 0, left_side, 0.0)
    right_side = jnp.where(position[None, :] != columns - 1, right_side, 0.0)
    return upper_row + lower_row + left_side + right_side - 4.0 * middle


def tendency(padded, columns, decay_rates, source, diffusion, saturation, off_diagonal, outflow):
    cell_count = decay_rates.shape[1]
    field_now = padded[:, columns:columns + cell_count]
    spread = laplace(padded, columns, cell_count)
    mixing = jnp.dot(off_diagonal, field_now, precision=precise)
    squared = field_now * field_now
    saturated = squared * field_now / (1.0 + squared)
    return (diffusion[:, None] * spread + mixing - (outflow[:, None] + decay_rates) * field_now
            - saturation[:, None] * saturated + source)


def jacobian(step_length, decay_rates, diffusion, off_diagonal, outflow):
    species = off_diagonal.shape[0]
    diagonal = 1.0 + step_length * (4.0 * diffusion[:, None] + outflow[:, None] + decay_rates)
    identity = jnp.eye(species, dtype=jnp.float32)
    return identity[:, :, None] * diagonal[None, :, :] - step_length * off_diagonal[:, :, None]


def invert(matrices):
    species = matrices.shape[0]
    numbers = jnp.arange(species, dtype=jnp.int32)

    def eliminate(pivot_index, current):
        pivot_row = lax.dynamic_index_in_dim(current, pivot_index, 0, keepdims=False)
        pivot_column = lax.dynamic_index_in_dim(current, pivot_index, 1, keepdims=False)
        pivot_value = lax.dynamic_index_in_dim(pivot_row, pivot_index, 0, keepdims=False)
        is_pivot = numbers == pivot_index
        scaled = jnp.where(is_pivot[:, None], 1.0, pivot_row) / pivot_value[None, :]
        weights = jnp.where(is_pivot[:, None], 0.0, pivot_column)
        cleared = jnp.where(is_pivot[None, :, None], 0.0, current)
        updated = cleared - weights[:, None, :] * scaled[None, :, :]
        return jnp.where(is_pivot[:, None, None], scaled[None, :, :], updated)

    return lax.fori_loop(0, species, eliminate, matrices)


def apply_inverse(inverse_table, vector):
    return jnp.einsum("ijc,jc->ic", inverse_table.astype(jnp.float32), vector, precision=precise)


def reference(initial_field, decay_rates, source, diffusion, saturation, conversion):
    off_diagonal, outflow = conversion_parts(conversion)
    fine_table = invert(jacobian(1.0, decay_rates, diffusion, off_diagonal, outflow)).astype(jnp.bfloat16)
    coarse_table = invert(jacobian(float(FACTOR), decay_rates, diffusion, off_diagonal, outflow)).astype(jnp.bfloat16)

    def force(field_now):
        padded = jnp.pad(field_now, ((0, 0), (COLS, COLS)))
        return tendency(padded, COLS, decay_rates, source, diffusion, saturation, off_diagonal, outflow)

    def fine_step(previous):
        iterate = previous
        for newton_turn in range(NEWTON):
            defect = iterate - previous - force(iterate)
            iterate = iterate - apply_inverse(fine_table, defect)
        return iterate

    def coarse_step(field_now):
        return field_now + FACTOR * apply_inverse(coarse_table, force(field_now))

    def propagate(field_now):
        for fine_turn in range(FACTOR):
            field_now = fine_step(field_now)
        return field_now

    points = jnp.broadcast_to(initial_field[None], (INTERVALS,) + initial_field.shape)
    for cycle_index in range(CYCLES):
        reached = jax.vmap(propagate)(points)
        points = jnp.concatenate([initial_field[None], reached[:-1]], axis=0)
        reached = jax.vmap(propagate)(points)
        defects = reached - jax.vmap(coarse_step)(points)

        def chain_link(carried, defect_now):
            advanced = coarse_step(carried) + defect_now
            return advanced, advanced

        last_point, following = lax.scan(chain_link, initial_field, defects[:-1])
        points = jnp.concatenate([initial_field[None], following], axis=0)
    return points
```

```python
import functools

import jax
import jax.numpy as jnp
from jax import lax
from jax.experimental import pallas as pl
from jax.experimental.pallas import tpu as pltpu
from jax.sharding import PartitionSpec as P

COLS = 128
FACTOR = 4
NEWTON = 2
ROWS = 16
CELLS = 2048
S = 48
TILE = 256
CENTRE = 0.4
ENOUGH = 2e-4
GROUP = 4

VMEM = pl.BlockSpec(memory_space=pltpu.VMEM)
ANY = pl.BlockSpec(memory_space=pl.ANY)
TILES = [slice(start, start + TILE) for start in range(0, CELLS, TILE)]
SMEM = pl.BlockSpec(memory_space=pltpu.SMEM)
PARAMS = pltpu.CompilerParams(vmem_limit_bytes=48 << 20)


def halves(value):
    high = value.astype(jnp.bfloat16)
    low = (value - high.astype(jnp.float32)).astype(jnp.bfloat16)
    return high, low


def stacked(value):
    high, low = halves(value)
    return jnp.concatenate([high, low, high], axis=0)


def wide(matrix):
    rounded = lax.reduce_precision(matrix, 8, 7)
    high, low = rounded.astype(jnp.bfloat16), (matrix - rounded).astype(jnp.bfloat16)
    return jnp.concatenate([high, high, low], axis=1)


def times(matrix, value):
    return jnp.dot(matrix, stacked(value), preferred_element_type=jnp.float32)


def invert_kernel(matrix_ref, out_ref, first_mode, second_mode):
    lane = lax.broadcasted_iota(jnp.int32, (S, COLS), 1)
    row_number = lax.broadcasted_iota(jnp.int32, (S, COLS), 0)
    lane_row = lax.broadcasted_iota(jnp.int32, (1, COLS), 1)
    out_ref[...] = matrix_ref[...]

    def eliminate(k, _):
        current = out_ref[...]
        row = out_ref[pl.ds(k, 1), :]
        first = jnp.sum(jnp.where(lane == k, current, 0.0), axis=1, keepdims=True)
        second = jnp.sum(jnp.where(lane == k + 64, current, 0.0), axis=1, keepdims=True)
        pivot_first = jnp.sum(jnp.where(lane_row == k, row, 0.0), axis=1, keepdims=True)
        pivot_second = jnp.sum(jnp.where(lane_row == k + 64, row, 0.0), axis=1, keepdims=True)
        column = jnp.where(lane < 64, first, second)
        pivot = jnp.where(lane_row < 64, pivot_first, pivot_second)
        at_row = (lane_row == k) | (lane_row == k + 64)
        scaled = jnp.where(at_row, 1.0, row) / pivot
        weights = jnp.where(row_number == k, 0.0, column)
        cleared = jnp.where((lane == k) | (lane == k + 64), 0.0, current)
        updated = cleared - weights * scaled
        out_ref[...] = jnp.where(row_number == k, scaled, updated)
        return 0

    lax.fori_loop(0, S, eliminate, 0)
    for at, mode in ((0, first_mode), (64, second_mode)):
        power = out_ref[:, at : at + S]
        for _ in range(2):
            power = jnp.dot(power, power, precision=lax.Precision.HIGHEST, preferred_element_type=jnp.float32)
        mode[...] = jnp.sum(power, axis=1, keepdims=True)


def invert_pair(first, second):
    gap = jnp.zeros((S, 16), jnp.float32)
    pair = jnp.concatenate([first, gap, second, gap], axis=1)
    pair = pair + jnp.where(jnp.arange(COLS) % 64 >= S, 1.0, 0.0)[None, :]
    column = jax.ShapeDtypeStruct((S, 1), jnp.float32)
    inverted, first_mode, second_mode = pl.pallas_call(
        invert_kernel,
        out_shape=[jax.ShapeDtypeStruct((S, COLS), jnp.float32), column, column],
        in_specs=[VMEM],
        out_specs=[VMEM] * 3,
        name="invert_pair",
    )(pair)
    return inverted[:, :S], inverted[:, 64 : 64 + S], first_mode, second_mode


class Solver:
    def __init__(self, inverse, mode, balance):
        self.inverse, self.balance = inverse, balance
        self.mode = jnp.broadcast_to(mode[...], (S, TILE))


class Grid:
    def __init__(self, rate, delta, source, spread, saturation, mixing, residual, change):
        self.rate, self.delta, self.source = rate, delta, source
        self.spread = jnp.broadcast_to(spread[...], (S, COLS))
        self.saturation = jnp.broadcast_to(saturation[...], (S, COLS))
        self.mixing, self.residual, self.change = mixing, residual, change
        lane = lax.broadcasted_iota(jnp.int32, (S, COLS), 1)
        self.not_first, self.not_last = lane != 0, lane != COLS - 1

    def force_row(self, field, r, mixed):
        at = slice(r * COLS, (r + 1) * COLS)
        here = field[:, at]
        around = jnp.where(self.not_first, pltpu.roll(here, 1, 1), 0.0) + jnp.where(
            self.not_last, pltpu.roll(here, COLS - 1, 1), 0.0
        )
        if r > 0:
            around = around + field[:, (r - 1) * COLS : r * COLS]
        if r < ROWS - 1:
            around = around + field[:, (r + 1) * COLS : (r + 2) * COLS]
        saturated = self.saturation * here / (1.0 + here * here)
        return self.spread * around + mixed - self.rate[:, at] * here + saturated + self.source[:, at]

    def force(self, field, at):
        mixed = times(self.mixing[...], field[:, at])
        r = at.start // COLS
        return jnp.concatenate(
            [self.force_row(field, r + k, mixed[:, k * COLS : (k + 1) * COLS]) for k in range(2)],
            axis=1,
        )

    def turn(self, solver, at, value, before):
        change = times(solver.inverse[...], value)
        left = self.delta[:, at] * (change if before is None else change - before)
        share = jnp.sum(left, axis=0, keepdims=True) * solver.balance[:, at]
        return change + solver.mode * share, left

    def solve(self, solver, field, previous, count, finish):
        for at in TILES:
            value = self.force(field, at)
            if previous is not None:
                value = value + (previous[:, at] - field[:, at])
            self.residual[:, at] = value
            self.change[:, at] = self.turn(solver, at, value, None)[0]

        def next_turn(at):
            before = self.change[:, at]
            return self.turn(solver, at, self.residual[:, at] + self.delta[:, at] * before, before)

        def middle(_, carry):
            for at in TILES:
                self.change[:, at] = next_turn(at)[0]
            return carry

        lax.fori_loop(2, count, middle, 0)
        for at in TILES:
            finish(at, *next_turn(at))

    def fine_steps(self, solver, field, previous, count):
        def first(at, change, _):
            here = field[:, at]
            previous[:, at] = here
            field[:, at] = here + change

        def second(at, change, _):
            field[:, at] = field[:, at] + change

        def step(_, carry):
            self.solve(solver, field, None, count, first)
            self.solve(solver, field, previous, count, second)
            return carry

        lax.fori_loop(0, FACTOR, step, 0)


def main_kernel(
    where, own, beside, across, corner, fine, coarse, fine_mode, coarse_mode,
    mixing, spread, saturation, still,
    half, rest, first, rate, delta, source, balance, counts,
    field, previous, keep, residual, change, fine_balance,
):
    interval, strip = where[0], where[1]
    width = own.shape[1]
    pieces = (own, beside, across, corner)

    def place(k):
        return pl.ds(pl.multiple_of(jnp.bitwise_xor(strip, k) * width, COLS), width)

    for k, piece in enumerate(pieces):
        decay = piece[S : 2 * S, :]
        delta[:, place(k)] = CENTRE - decay
        rate[:, place(k)] = still[...] + decay
        source[:, place(k)] = piece[2 * S : 3 * S, :]
        for mode, shift, total in ((fine_mode, 1.0, fine_balance), (coarse_mode, 1.0 / FACTOR, balance)):
            losses = (shift + 4.0 * spread[...] + decay) * mode[...]
            total[:, place(k)] = 1.0 / jnp.sum(losses, axis=0, keepdims=True)
    grid = Grid(rate, delta, source, spread, saturation, mixing, residual, change)
    fine_solver = Solver(fine, fine_mode, fine_balance)
    coarse_solver = Solver(coarse, coarse_mode, balance)

    def own_strip():
        return field[:, pl.ds(pl.multiple_of(strip * width, COLS), width)]

    def attempt(state):
        fine_count, coarse_count = 2 << state[0], 3 << state[0]
        counts[0], counts[1] = fine_count, coarse_count
        for k, piece in enumerate(pieces):
            field[:, place(k)] = piece[0:S, :]
        first[0] = own_strip()
        grid.fine_steps(fine_solver, field, previous, fine_count)
        first[1] = own_strip()
        for at in TILES:
            keep[:, at] = field[:, at]
        grid.fine_steps(fine_solver, field, previous, fine_count)
        first[2] = own_strip()
        errors, squares = [], []

        def defect(at, moved, left):
            here = field[:, at]
            rest_of = here - keep[:, at] - moved
            previous[:, at] = rest_of
            errors.append(left * left)
            squares.append(here * here)

        grid.solve(coarse_solver, keep, None, coarse_count, defect)
        error, square = jnp.sum(sum(errors)), jnp.sum(sum(squares))
        return state[0] + 1, error <= (ENOUGH * ENOUGH) * square

    lax.while_loop(lambda state: jnp.logical_not(state[1]) & (state[0] < 6), attempt, (jnp.int32(0), False))
    fine_count, coarse_count = counts[0], counts[1]

    @pl.when(interval <= 3)
    def _():
        for at in TILES:
            field[:, at] = keep[:, at]

    for at in TILES:
        keep[:, at] = previous[:, at]

    def linked(at, moved, _):
        field[:, at] = field[:, at] + moved + keep[:, at]

    def link(_, carry):
        grid.solve(coarse_solver, field, None, coarse_count, linked)
        return carry

    lax.fori_loop(4, interval, link, 0)
    grid.fine_steps(fine_solver, field, previous, fine_count)
    for at in TILES:
        keep[:, at] = field[:, at]
    grid.fine_steps(fine_solver, field, previous, fine_count)

    def handed(at, moved, _):
        previous[:, at] = field[:, at] - jnp.where(interval <= 3, 0.0, keep[:, at] + moved)

    grid.solve(coarse_solver, keep, None, coarse_count, handed)
    half[...] = previous[:, half_at(strip, 0)]
    rest[...] = previous[:, half_at(strip, 1)]


def half_at(strip, other):
    core = jnp.bitwise_xor(jnp.bitwise_and(strip, 1), other)
    return pl.ds(pl.multiple_of(core * (CELLS // 2), COLS), CELLS // 2)


def whole():
    return jax.ShapeDtypeStruct((S, CELLS), jnp.float32)


def half_grid():
    return jax.ShapeDtypeStruct((S, CELLS // 2), jnp.float32)


def line():
    return jax.ShapeDtypeStruct((1, CELLS), jnp.float32)


def scratch(count):
    return [pltpu.VMEM((S, CELLS), jnp.float32) for _ in range(count)]


def run_main(where, pieces, *shared):
    width = pieces[0].shape[1]
    return pl.pallas_call(
        main_kernel,
        out_shape=[
            half_grid(), half_grid(), jax.ShapeDtypeStruct((3, S, width), jnp.float32),
            whole(), whole(), whole(), line(), jax.ShapeDtypeStruct((2,), jnp.int32),
        ],
        in_specs=[SMEM] + [VMEM] * 12,
        out_specs=[VMEM] * 7 + [SMEM],
        scratch_shapes=scratch(5) + [pltpu.VMEM((1, CELLS), jnp.float32)],
        compiler_params=PARAMS,
        name="to_payload",
    )(where, *pieces, *shared)


def chain_kernel(*refs):
    where, counts = refs[:2]
    arrived, payloads = refs[2:4], refs[4 : 4 + 2 * GROUP]
    rest = refs[4 + 2 * GROUP :]
    coefficients = rest[:3]
    coarse, mode, balance, mixing, spread, saturation = rest[3:9]
    half, mine, field, residual, change, rate, delta, source, stage, fetched, passed = rest[9:]
    member, strip = where[0] % GROUP, where[1]
    width = mine.shape[1]
    copies = [pltpu.make_async_copy(arrived[k], field.at[:, half_at(strip, k)], fetched.at[k]) for k in range(2)]
    copies += [
        pltpu.make_async_copy(source_ref, target, fetched.at[2 + k])
        for k, (source_ref, target) in enumerate(zip(coefficients, (rate, delta, source)))
    ]
    held = []
    for j in range(GROUP):
        slot = (member + j) % GROUP
        held.append([
            pltpu.make_async_copy(
                payloads[2 * j + k], stage.at[slot, :, half_at(strip, k)], passed.at[slot, k]
            )
            for k in range(2)
        ])
    for copy in copies + sum(held, []):
        copy.start()
    for copy in copies:
        copy.wait()
    grid = Grid(rate, delta, source, spread, saturation, mixing, residual, change)
    solver = Solver(coarse, mode, balance)
    for pair in held:
        for copy in pair:
            copy.wait()

    def link(k, carry):
        def linked(at, moved, _):
            field[:, at] = field[:, at] + moved + stage[k, :, at]

        grid.solve(solver, field, None, counts[1], linked)

        @pl.when(member == k)
        def _():
            mine[...] = field[:, pl.ds(pl.multiple_of(strip * width, COLS), width)]

        return carry

    lax.fori_loop(0, GROUP, link, 0)
    half[...] = field[:, half_at(strip, 0)]


def run_chain(where, counts, arrived, payloads, coefficients, shared):
    return pl.pallas_call(
        chain_kernel,
        out_shape=[half_grid(), jax.ShapeDtypeStruct((S, CELLS // 4), jnp.float32)],
        in_specs=[SMEM, SMEM] + [ANY] * (2 + 2 * GROUP + 3) + [VMEM] * 6,
        out_specs=[VMEM, VMEM],
        scratch_shapes=scratch(6)
        + [
            pltpu.VMEM((GROUP, S, CELLS), jnp.float32),
            pltpu.SemaphoreType.DMA((5,)),
            pltpu.SemaphoreType.DMA((GROUP, 2)),
        ],
        compiler_params=PARAMS,
        name="links",
    )(where, counts, *arrived, *payloads, *coefficients, *shared)


def neighbour_route():
    route = []
    for tm in range(32):
        for strip in range(4):
            high, low, core = (tm // 4) % 2, strip // 2, strip % 2
            y = high * 2 + low
            from_y = (y + 1) % 4 if core else (y - 1) % 4
            from_tm = tm + ((from_y // 2) - high) * 4
            route.append((from_tm * 4 + (from_y % 2) * 2 + core, tm * 4 + strip))
    return route


def per_device(initial_field, decay_rates, source, diffusion, saturation, conversion):
    strip, interval = lax.axis_index("space"), lax.axis_index("tm")
    where = jnp.stack([interval, strip]).astype(jnp.int32)
    own = jnp.concatenate([initial_field, decay_rates, source], axis=0)
    swap = [(0, 1), (1, 0), (2, 3), (3, 2)]
    across = lax.ppermute(own, ("tm", "space"), neighbour_route())
    beside = lax.ppermute(own, "space", swap)
    corner = lax.ppermute(across, "space", swap)

    off_diagonal = conversion * (1.0 - jnp.eye(S, dtype=jnp.float32))
    outflow = jnp.sum(off_diagonal, axis=0)
    still = 4.0 * diffusion + outflow
    centre = jnp.eye(S, dtype=jnp.float32) * (still + CENTRE)[:, None] - off_diagonal
    fine, coarse, fine_mode, coarse_mode = invert_pair(
        centre + jnp.eye(S, dtype=jnp.float32), centre + jnp.eye(S, dtype=jnp.float32) / FACTOR
    )
    fine, coarse, mixing = wide(fine), wide(coarse), wide(off_diagonal)
    spread, saturation, still = diffusion[:, None], saturation[:, None], (still + saturation)[:, None]
    half, rest, first, *coefficients, balance, counts = run_main(
        where, (own, beside, across, corner), fine, coarse, fine_mode, coarse_mode,
        mixing, spread, saturation, still,
    )
    shared = (coarse, coarse_mode, balance, mixing, spread, saturation)
    in_group = [half, rest]
    for distance in range(1, GROUP):
        route = [(i // GROUP * GROUP + (i + distance) % GROUP, i) for i in range(32)]
        arrived = lax.ppermute(half, "tm", route)
        in_group += [arrived, lax.ppermute(arrived, "space", swap)]
    group, member = interval // GROUP, interval % GROUP
    last = half
    for j in range(1, GROUP):
        last = jnp.where((member + j) % GROUP == GROUP - 1, in_group[2 * j], last)
    width = initial_field.shape[1]
    both = jnp.where(strip % 2 == strip // 2, half, rest)
    third = lax.dynamic_slice_in_dim(both, (strip % 2) * width, width, axis=1)
    mine = jnp.where(
        interval == 0, first[0], jnp.where(interval == 1, first[1], jnp.where(interval == 2, first[2], third))
    )
    for hop in range(32 // GROUP - 1):
        route = [(hop * GROUP + m, (hop + 1) * GROUP + m) for m in range(GROUP)]
        arrived = lax.ppermute(last, "tm", route)
        arrived = (arrived, lax.ppermute(arrived, "space", swap))

        def active(arrived=arrived):
            return tuple(run_chain(where, counts, arrived, in_group, coefficients, shared))

        last, mine = lax.cond(group == hop + 1, active, lambda: (last, mine))
    return mine[None]


def solution(mesh):
    in_specs = (P(None, "space"), P(None, "space"), P(None, "space"), P(), P(), P())
    out_specs = P("tm", None, "space")
    return jax.shard_map(
        per_device, mesh=mesh, in_specs=in_specs, out_specs=out_specs, check_vma=False
    )
```

```python
import functools

import jax
import jax.numpy as jnp
from jax import lax
from jax.experimental import pallas as pl
from jax.experimental.pallas import tpu as pltpu
from jax.sharding import PartitionSpec as P

COLS = 128
FACTOR = 4
NEWTON = 2
ROWS = 16
CELLS = 2048
S = 48
TILE = 256
CENTRE = 0.4
ENOUGH = 2.5e-4

VMEM = pl.BlockSpec(memory_space=pltpu.VMEM)
ANY = pl.BlockSpec(memory_space=pl.ANY)
TILES = [slice(start, start + TILE) for start in range(0, CELLS, TILE)]
SMEM = pl.BlockSpec(memory_space=pltpu.SMEM)
PARAMS = pltpu.CompilerParams(vmem_limit_bytes=48 << 20)


def halves(value):
    high = value.astype(jnp.bfloat16)
    low = (value - high.astype(jnp.float32)).astype(jnp.bfloat16)
    return high, low


def stacked(value):
    high, low = halves(value)
    return jnp.concatenate([high, low, high], axis=0)


def wide(matrix):
    rounded = lax.reduce_precision(matrix, 8, 7)
    high, low = rounded.astype(jnp.bfloat16), (matrix - rounded).astype(jnp.bfloat16)
    return jnp.concatenate([high, high, low], axis=1)


def times(matrix, value):
    return jnp.dot(matrix, stacked(value), preferred_element_type=jnp.float32)


def invert_kernel(matrix_ref, out_ref, first_mode, second_mode):
    lane = lax.broadcasted_iota(jnp.int32, (S, COLS), 1)
    row_number = lax.broadcasted_iota(jnp.int32, (S, COLS), 0)
    lane_row = lax.broadcasted_iota(jnp.int32, (1, COLS), 1)
    out_ref[...] = matrix_ref[...]

    def eliminate(k, _):
        current = out_ref[...]
        row = out_ref[pl.ds(k, 1), :]
        first = jnp.sum(jnp.where(lane == k, current, 0.0), axis=1, keepdims=True)
        second = jnp.sum(jnp.where(lane == k + 64, current, 0.0), axis=1, keepdims=True)
        pivot_first = jnp.sum(jnp.where(lane_row == k, row, 0.0), axis=1, keepdims=True)
        pivot_second = jnp.sum(jnp.where(lane_row == k + 64, row, 0.0), axis=1, keepdims=True)
        column = jnp.where(lane < 64, first, second)
        pivot = jnp.where(lane_row < 64, pivot_first, pivot_second)
        at_row = (lane_row == k) | (lane_row == k + 64)
        scaled = jnp.where(at_row, 1.0, row) / pivot
        weights = jnp.where(row_number == k, 0.0, column)
        cleared = jnp.where((lane == k) | (lane == k + 64), 0.0, current)
        updated = cleared - weights * scaled
        out_ref[...] = jnp.where(row_number == k, scaled, updated)
        return 0

    lax.fori_loop(0, S, eliminate, 0)
    for at, mode in ((0, first_mode), (64, second_mode)):
        power = out_ref[:, at : at + S]
        for _ in range(2):
            power = jnp.dot(power, power, precision=lax.Precision.HIGHEST, preferred_element_type=jnp.float32)
        mode[...] = jnp.sum(power, axis=1, keepdims=True)


def invert_pair(first, second):
    gap = jnp.zeros((S, 16), jnp.float32)
    pair = jnp.concatenate([first, gap, second, gap], axis=1)
    pair = pair + jnp.where(jnp.arange(COLS) % 64 >= S, 1.0, 0.0)[None, :]
    column = jax.ShapeDtypeStruct((S, 1), jnp.float32)
    inverted, first_mode, second_mode = pl.pallas_call(
        invert_kernel,
        out_shape=[jax.ShapeDtypeStruct((S, COLS), jnp.float32), column, column],
        in_specs=[VMEM],
        out_specs=[VMEM] * 3,
        name="invert_pair",
    )(pair)
    return inverted[:, :S], inverted[:, 64 : 64 + S], first_mode, second_mode


class Solver:
    def __init__(self, inverse, mode, balance, shift, turns, early):
        self.inverse, self.balance, self.shift = inverse, balance, shift
        self.turns, self.early = turns, early
        self.mode = jnp.broadcast_to(mode[...], (S, TILE))


class Grid:
    def __init__(self, delta, source, spread, saturation, base, change):
        self.delta, self.source = delta, source
        self.spread = jnp.broadcast_to(spread[...], (S, COLS))
        self.saturation = jnp.broadcast_to(saturation[...], (S, COLS))
        self.base, self.change = base, change
        lane = lax.broadcasted_iota(jnp.int32, (S, COLS), 1)
        self.not_first, self.not_last = lane != 0, lane != COLS - 1

    def driven(self, field, r):
        at = slice(r * COLS, (r + 1) * COLS)
        here = field[:, at]
        around = jnp.where(self.not_first, pltpu.roll(here, 1, 1), 0.0) + jnp.where(
            self.not_last, pltpu.roll(here, COLS - 1, 1), 0.0
        )
        if r > 0:
            around = around + field[:, (r - 1) * COLS : r * COLS]
        if r < ROWS - 1:
            around = around + field[:, (r + 1) * COLS : (r + 2) * COLS]
        saturated = self.saturation * (here / (1.0 + here * here) - here)
        return self.spread * around + self.delta[:, at] * here + saturated + self.source[:, at]

    def share(self, solver, at, left):
        return solver.mode * (jnp.sum(left, axis=0, keepdims=True) * solver.balance[:, at])

    def first_turn(self, solver, field, previous, at):
        r = at.start // COLS
        here = field[:, at]
        value = jnp.concatenate([self.driven(field, r + k) for k in range(2)], axis=1)
        value = value + (solver.shift * here if previous is None else previous[:, at])
        base = times(solver.inverse[...], value) - here
        if solver.early:
            return base, base + self.share(solver, at, self.delta[:, at] * base)
        return base, base

    def next_turn(self, solver, at, base, before):
        change = base + times(solver.inverse[...], self.delta[:, at] * before)
        left = self.delta[:, at] * (change - before)
        return change + self.share(solver, at, left), left

    def solve(self, solver, field, previous, level, finish):
        def first(at):
            return self.first_turn(solver, field, previous, at)

        def last(at, base, change):
            finish(at, *self.next_turn(solver, at, base, change))

        def middle(at):
            return self.next_turn(solver, at, self.base[:, at], self.change[:, at])[0]

        if solver.turns == 2:

            @pl.when(level == 0)
            def _():
                for at in TILES:
                    last(at, *first(at))

            @pl.when(level > 0)
            def _():
                for at in TILES:
                    self.base[:, at], self.change[:, at] = first(at)

                def again(_, carry):
                    for at in TILES:
                        self.change[:, at] = middle(at)
                    return carry

                lax.fori_loop(2, 2 << level, again, 0)
                for at in TILES:
                    last(at, self.base[:, at], self.change[:, at])

        else:
            for at in TILES:
                self.base[:, at], self.change[:, at] = first(at)

            @pl.when(level == 0)
            def _():
                for at in TILES:
                    last(at, self.base[:, at], middle(at))

            @pl.when(level > 0)
            def _():
                def pair(_, carry):
                    for at in TILES:
                        change, left = self.next_turn(solver, at, self.base[:, at], middle(at))
                        self.change[:, at] = change
                        finish(at, change, left)
                    return carry

                lax.fori_loop(0, (1 << level) + (1 << level) // 2, pair, 0)

    def fine_steps(self, solver, field, middle, level):
        def first(at, change, _):
            middle[:, at] = field[:, at] + change

        def second(at, change, _):
            field[:, at] = middle[:, at] + change

        def step(_, carry):
            self.solve(solver, field, None, level, first)
            self.solve(solver, middle, field, level, second)
            return carry

        lax.fori_loop(0, FACTOR, step, 0)


def main_kernel(
    where, own, beside, across, corner, fine, coarse, fine_mode, coarse_mode,
    spread, saturation,
    half, rest, mine, delta, source, balance, counts,
    field, middle, keep, base, change, errors, squares, fine_balance,
):
    interval, strip = where[0], where[1]
    width = own.shape[1]
    pieces = (own, beside, across, corner)

    def place(k):
        return pl.ds(pl.multiple_of(jnp.bitwise_xor(strip, k) * width, COLS), width)

    for k, piece in enumerate(pieces):
        decay = piece[S : 2 * S, :]
        delta[:, place(k)] = CENTRE - decay
        source[:, place(k)] = piece[2 * S : 3 * S, :]
        for mode, shift, total in ((fine_mode, 1.0, fine_balance), (coarse_mode, 1.0 / FACTOR, balance)):
            losses = (shift + 4.0 * spread[...] + decay) * mode[...]
            total[:, place(k)] = 1.0 / jnp.sum(losses, axis=0, keepdims=True)
    grid = Grid(delta, source, spread, saturation, base, change)
    fine_solver = Solver(fine, fine_mode, fine_balance, 1.0, 2, False)
    coarse_solver = Solver(coarse, coarse_mode, balance, 1.0 / FACTOR, 3, True)

    def keep_own(condition):
        @pl.when(condition)
        def _():
            mine[...] = field[:, pl.ds(pl.multiple_of(strip * width, COLS), width)]

    def attempt(state):
        level = state[0]
        counts[0] = level
        for k, piece in enumerate(pieces):
            field[:, place(k)] = piece[0:S, :]
        keep_own(interval == 0)

        def interval_steps(phase, carry):
            for at in TILES:
                keep[:, at] = field[:, at]
            grid.fine_steps(fine_solver, field, middle, level)
            keep_own(interval == phase + 1)
            return carry

        lax.fori_loop(0, 2, interval_steps, 0)

        def defect(at, moved, left):
            here = field[:, at]
            middle[:, at] = here - keep[:, at] - moved
            errors[:, at] = left * left
            squares[:, at] = here * here

        grid.solve(coarse_solver, keep, None, level, defect)
        return level + 1, jnp.sum(errors[...]) <= (ENOUGH * ENOUGH) * jnp.sum(squares[...])

    lax.while_loop(lambda state: jnp.logical_not(state[1]) & (state[0] < 6), attempt, (jnp.int32(0), False))
    level = counts[0]

    @pl.when(interval <= 3)
    def _():
        for at in TILES:
            field[:, at] = keep[:, at]

    for at in TILES:
        keep[:, at] = middle[:, at]

    def linked(at, moved, _):
        middle[:, at] = field[:, at] + moved + keep[:, at]

    def link(_, carry):
        grid.solve(coarse_solver, field, None, level, linked)
        for at in TILES:
            field[:, at] = middle[:, at]
        return carry

    lax.fori_loop(4, interval, link, 0)

    def interval_steps(_, carry):
        for at in TILES:
            keep[:, at] = field[:, at]
        grid.fine_steps(fine_solver, field, middle, level)
        return carry

    lax.fori_loop(0, 2, interval_steps, 0)

    def handed(at, moved, _):
        middle[:, at] = field[:, at] - jnp.where(interval <= 4, 0.0, keep[:, at] + moved)

    grid.solve(coarse_solver, keep, None, level, handed)
    keep_own((interval == 3) | (interval == 4))
    half[...] = middle[:, half_at(strip, 0)]
    rest[...] = middle[:, half_at(strip, 1)]


def half_at(strip, other):
    core = jnp.bitwise_xor(jnp.bitwise_and(strip, 1), other)
    return pl.ds(pl.multiple_of(core * (CELLS // 2), COLS), CELLS // 2)


def whole():
    return jax.ShapeDtypeStruct((S, CELLS), jnp.float32)


def half_grid():
    return jax.ShapeDtypeStruct((S, CELLS // 2), jnp.float32)


def line():
    return jax.ShapeDtypeStruct((1, CELLS), jnp.float32)


def scratch(count):
    return [pltpu.VMEM((S, CELLS), jnp.float32) for _ in range(count)]


def run_main(where, pieces, *shared):
    width = pieces[0].shape[1]
    return pl.pallas_call(
        main_kernel,
        out_shape=[
            half_grid(), half_grid(), jax.ShapeDtypeStruct((S, width), jnp.float32),
            whole(), whole(), line(), jax.ShapeDtypeStruct((1,), jnp.int32),
        ],
        in_specs=[SMEM] + [VMEM] * 10,
        out_specs=[VMEM] * 6 + [SMEM],
        scratch_shapes=scratch(7) + [pltpu.VMEM((1, CELLS), jnp.float32)],
        compiler_params=PARAMS,
        name="to_payload",
    )(where, *pieces, *shared)


def slot_of(member, core, j):
    near = jnp.bitwise_xor(member, jnp.where(core == 0, (0, 1, 3, 2)[j % 4], (0, 3, 1, 2)[j % 4]))
    return jnp.bitwise_xor(near, j // 4 * 4)


def chain_kernel(length, seeded, *refs):
    where, counts = refs[:2]
    arrived, payloads = refs[2:4], refs[4 : 4 + 2 * length]
    rest = refs[4 + 2 * length :]
    coefficients = rest[:2]
    coarse, mode, balance, spread, saturation = rest[2:7]
    half, mine, field, middle, base, change, delta, source, stage, fetched, passed = rest[7:]
    member, strip = where[0] % length, where[1]
    width = mine.shape[1]

    def held(piece, slot, k):
        return pltpu.make_async_copy(piece, stage.at[slot, :, half_at(strip, k)], passed.at[slot, k])

    copies = [] if seeded else [pltpu.make_async_copy(arrived[k], field.at[:, half_at(strip, k)], fetched.at[k]) for k in range(2)]
    copies += [
        pltpu.make_async_copy(source_ref, target, fetched.at[2 + k])
        for k, (source_ref, target) in enumerate(zip(coefficients, (delta, source)))
    ]
    for copy in copies:
        copy.start()
    for j in range(length):
        for k in range(2):
            core = jnp.bitwise_xor(jnp.bitwise_and(strip, 1), k)
            held(payloads[2 * j + k], slot_of(member, core, j), k).start()
    for copy in copies:
        copy.wait()
    grid = Grid(delta, source, spread, saturation, base, change)
    solver = Solver(coarse, mode, balance, 1.0 / FACTOR, 3, True)

    def show(slot, state):
        @pl.when(member == slot)
        def _():
            mine[...] = state[:, pl.ds(pl.multiple_of(strip * width, COLS), width)]

    def fetched_payload(slot):
        for k in range(2):
            held(payloads[k], slot, k).wait()

    def link(slot, carry):
        fetched_payload(slot)

        def linked(at, moved, _):
            middle[:, at] = field[:, at] + moved + stage[slot, :, at]

        grid.solve(solver, field, None, counts[0], linked)
        for at in TILES:
            field[:, at] = middle[:, at]
        show(slot, field)
        return carry

    if seeded:
        fetched_payload(0)
        field[...] = stage[0]
        show(0, field)
    lax.fori_loop(1 if seeded else 0, length, link, 0)
    half[...] = field[:, half_at(strip, 0)]


def run_chain(where, counts, arrived, payloads, coefficients, shared):
    length, seeded = len(payloads) // 2, arrived is None
    arrived = payloads[:2] if seeded else arrived
    return pl.pallas_call(
        functools.partial(chain_kernel, length, seeded),
        out_shape=[half_grid(), jax.ShapeDtypeStruct((S, CELLS // 4), jnp.float32)],
        in_specs=[SMEM, SMEM] + [ANY] * (2 + 2 * length + 2) + [VMEM] * 5,
        out_specs=[VMEM, VMEM],
        scratch_shapes=scratch(6)
        + [
            pltpu.VMEM((length, S, CELLS), jnp.float32),
            pltpu.SemaphoreType.DMA((4,)),
            pltpu.SemaphoreType.DMA((length, 2)),
        ],
        compiler_params=PARAMS,
        name=f"links_{length - seeded}",
    )(where, counts, *arrived, *payloads, *coefficients, *shared)


def neighbour_route():
    route = []
    for tm in range(32):
        for strip in range(4):
            high, low, core = (tm // 4) % 2, strip // 2, strip % 2
            y = high * 2 + low
            from_y = (y + 1) % 4 if core else (y - 1) % 4
            from_tm = tm + ((from_y // 2) - high) * 4
            route.append((from_tm * 4 + (from_y % 2) * 2 + core, tm * 4 + strip))
    return route


def per_device(initial_field, decay_rates, source, diffusion, saturation, conversion):
    strip, interval = lax.axis_index("space"), lax.axis_index("tm")
    where = jnp.stack([interval, strip]).astype(jnp.int32)
    own = jnp.concatenate([initial_field, decay_rates, source], axis=0)
    swap = [(0, 1), (1, 0), (2, 3), (3, 2)]
    across = lax.ppermute(own, ("tm", "space"), neighbour_route())
    beside = lax.ppermute(own, "space", swap)
    corner = lax.ppermute(across, "space", swap)

    off_diagonal = conversion * (1.0 - jnp.eye(S, dtype=jnp.float32))
    outflow = jnp.sum(off_diagonal, axis=0)
    still = 4.0 * diffusion + outflow
    centre = jnp.eye(S, dtype=jnp.float32) * (still + CENTRE)[:, None] - off_diagonal
    fine, coarse, fine_mode, coarse_mode = invert_pair(
        centre + jnp.eye(S, dtype=jnp.float32), centre + jnp.eye(S, dtype=jnp.float32) / FACTOR
    )
    fine, coarse = wide(fine), wide(coarse)
    spread, saturation = diffusion[:, None], saturation[:, None]
    half, rest, mine, *coefficients, balance, counts = run_main(
        where, (own, beside, across, corner), fine, coarse, fine_mode, coarse_mode, spread, saturation
    )
    shared = (coarse, coarse_mode, balance, spread, saturation)
    def swapped(piece):
        return [piece, lax.ppermute(piece, "space", swap)]

    def exchanged(piece, flips, lowest):
        route = [(4 * (i ^ flips[c % 2]) + c, 4 * i + c) for i in range(lowest, 32) for c in range(4)]
        return lax.ppermute(piece, ("tm", "space"), route)

    def doubled(piece, lowest):
        second = exchanged(piece, (1, 3), lowest)
        return [second, exchanged(piece, (3, 1), lowest), exchanged(second, (3, 1), lowest)]

    near = sum([swapped(piece) for piece in doubled(half, 4)], [half, rest])

    def advance(active, arrived, payloads, last, mine):
        def run():
            return tuple(run_chain(where, counts, arrived, payloads, coefficients, shared))

        return lax.cond(active, run, lambda: (last, mine))

    def hop(last, start, distance, length):
        return lax.ppermute(last, "tm", [(start - distance + m, start + m) for m in range(length)])

    last, mine = advance(interval // 4 == 1, None, near, half, mine)
    behind, last = lax.optimization_barrier((half, last))
    partner = swapped(lax.ppermute(behind, "tm", [(i ^ 4, i) for i in range(16, 32)]))
    payloads = near + partner + sum([swapped(piece) for piece in doubled(partner[0], 16)], [])
    for quarter in (2, 3):
        arrived = swapped(hop(last, 4 * quarter, 4, 4))
        last, mine = advance(interval // 4 == quarter, arrived, near, last, mine)
    arrived = jnp.where(interval // 4 == 4, hop(last, 16, 4, 4), hop(last, 20, 8, 4))
    last, mine = advance(interval // 8 == 2, swapped(arrived), payloads, last, mine)
    arrived = hop(last, 24, 8, 8)
    last, mine = advance(interval // 8 == 3, swapped(arrived), payloads, last, mine)
    return mine[None]


def solution(mesh):
    in_specs = (P(None, "space"), P(None, "space"), P(None, "space"), P(), P(), P())
    out_specs = P("tm", None, "space")
    return jax.shard_map(
        per_device, mesh=mesh, in_specs=in_specs, out_specs=out_specs, check_vma=False
    )
```

```python
import functools

import jax
import jax.numpy as jnp
from jax import lax
from jax.experimental import pallas as pl
from jax.experimental.pallas import tpu as pltpu
from jax.sharding import PartitionSpec as P

COLS = 128
FACTOR = 4
NEWTON = 2
ROWS = 16
CELLS = 2048
S = 48
TILE = 256
CENTRE = 0.4
ENOUGH = 2.5e-4

VMEM = pl.BlockSpec(memory_space=pltpu.VMEM)
ANY = pl.BlockSpec(memory_space=pl.ANY)
TILES = [slice(start, start + TILE) for start in range(0, CELLS, TILE)]
SMEM = pl.BlockSpec(memory_space=pltpu.SMEM)
PARAMS = pltpu.CompilerParams(vmem_limit_bytes=48 << 20)


def halves(value):
    high = value.astype(jnp.bfloat16)
    low = (value - high.astype(jnp.float32)).astype(jnp.bfloat16)
    return high, low


def stacked(value):
    high, low = halves(value)
    return jnp.concatenate([high, low, high], axis=0)


def wide(matrix):
    rounded = lax.reduce_precision(matrix, 8, 7)
    high, low = rounded.astype(jnp.bfloat16), (matrix - rounded).astype(jnp.bfloat16)
    return jnp.concatenate([high, high, low], axis=1)


def times(matrix, value):
    return jnp.dot(matrix, stacked(value), preferred_element_type=jnp.float32)


def invert_kernel(matrix_ref, out_ref, first_mode, second_mode):
    lane = lax.broadcasted_iota(jnp.int32, (S, COLS), 1)
    row_number = lax.broadcasted_iota(jnp.int32, (S, COLS), 0)
    lane_row = lax.broadcasted_iota(jnp.int32, (1, COLS), 1)
    out_ref[...] = matrix_ref[...]

    def taken(values, numbers, number):
        return jnp.sum(jnp.where(numbers == number, values, 0.0), axis=1, keepdims=True)

    def both(numbers, first, second):
        return jnp.where(numbers < 64, first, second)

    def eliminate(turn, _):
        k = 2 * turn
        current = out_ref[...]
        rows = [out_ref[pl.ds(k + p, 1), :] for p in range(2)]
        columns = [
            both(lane, taken(current, lane, k + p), taken(current, lane, k + 64 + p)) for p in range(2)
        ]
        block = [
            [both(lane_row, taken(row, lane_row, k + p), taken(row, lane_row, k + 64 + p)) for p in range(2)]
            for row in rows
        ]
        scale = 1.0 / (block[0][0] * block[1][1] - block[0][1] * block[1][0])
        at = [(lane_row == k + p) | (lane_row == k + 64 + p) for p in range(2)]
        either = at[0] | at[1]
        freed = [jnp.where(either, jnp.where(at[p], 1.0, 0.0), rows[p]) for p in range(2)]
        scaled = [
            scale * (block[1][1] * freed[0] - block[0][1] * freed[1]),
            scale * (block[0][0] * freed[1] - block[1][0] * freed[0]),
        ]
        updated = jnp.where(either, 0.0, current) - columns[0] * scaled[0] - columns[1] * scaled[1]
        for p in range(2):
            updated = jnp.where(row_number == k + p, scaled[p], updated)
        out_ref[...] = updated
        return 0

    lax.fori_loop(0, S // 2, eliminate, 0)
    for at, mode in ((0, first_mode), (64, second_mode)):
        power = out_ref[:, at : at + S]
        for _ in range(2):
            power = jnp.dot(power, power, precision=lax.Precision.HIGHEST, preferred_element_type=jnp.float32)
        mode[...] = jnp.sum(power, axis=1, keepdims=True)


def invert_pair(first, second):
    gap = jnp.zeros((S, 16), jnp.float32)
    pair = jnp.concatenate([first, gap, second, gap], axis=1)
    pair = pair + jnp.where(jnp.arange(COLS) % 64 >= S, 1.0, 0.0)[None, :]
    column = jax.ShapeDtypeStruct((S, 1), jnp.float32)
    inverted, first_mode, second_mode = pl.pallas_call(
        invert_kernel,
        out_shape=[jax.ShapeDtypeStruct((S, COLS), jnp.float32), column, column],
        in_specs=[VMEM],
        out_specs=[VMEM] * 3,
        name="invert_pair",
    )(pair)
    return inverted[:, :S], inverted[:, 64 : 64 + S], first_mode, second_mode


class Solver:
    def __init__(self, inverse, mode, balance, shift, turns, early):
        self.inverse, self.balance, self.shift = inverse, balance, shift
        self.turns, self.early = turns, early
        self.mode = jnp.broadcast_to(mode[...], (S, TILE))


class Grid:
    def __init__(self, delta, source, spread, saturation, base, change):
        self.delta, self.source = delta, source
        self.spread = jnp.broadcast_to(spread[...], (S, COLS))
        self.saturation = jnp.broadcast_to(saturation[...], (S, COLS))
        self.base, self.change = base, change
        lane = lax.broadcasted_iota(jnp.int32, (S, COLS), 1)
        self.not_first, self.not_last = lane != 0, lane != COLS - 1

    def driven(self, field, r):
        at = slice(r * COLS, (r + 1) * COLS)
        here = field[:, at]
        around = jnp.where(self.not_first, pltpu.roll(here, 1, 1), 0.0) + jnp.where(
            self.not_last, pltpu.roll(here, COLS - 1, 1), 0.0
        )
        if r > 0:
            around = around + field[:, (r - 1) * COLS : r * COLS]
        if r < ROWS - 1:
            around = around + field[:, (r + 1) * COLS : (r + 2) * COLS]
        saturated = self.saturation * (here / (1.0 + here * here) - here)
        return self.spread * around + self.delta[:, at] * here + saturated + self.source[:, at]

    def share(self, solver, at, left):
        return solver.mode * (jnp.sum(left, axis=0, keepdims=True) * solver.balance[:, at])

    def first_turn(self, solver, field, previous, at):
        r = at.start // COLS
        here = field[:, at]
        value = jnp.concatenate([self.driven(field, r + k) for k in range(2)], axis=1)
        value = value + (solver.shift * here if previous is None else previous[:, at])
        base = times(solver.inverse[...], value) - here
        if solver.early:
            return base, base + self.share(solver, at, self.delta[:, at] * base)
        return base, base

    def next_turn(self, solver, at, base, before):
        change = base + times(solver.inverse[...], self.delta[:, at] * before)
        left = self.delta[:, at] * (change - before)
        return change + self.share(solver, at, left), left

    def solve(self, solver, field, previous, level, finish):
        def first(at):
            return self.first_turn(solver, field, previous, at)

        def last(at, base, change):
            finish(at, *self.next_turn(solver, at, base, change))

        def middle(at):
            return self.next_turn(solver, at, self.base[:, at], self.change[:, at])[0]

        if solver.turns == 2:

            @pl.when(level == 0)
            def _():
                for at in TILES:
                    last(at, *first(at))

            @pl.when(level > 0)
            def _():
                for at in TILES:
                    self.base[:, at], self.change[:, at] = first(at)

                def again(_, carry):
                    for at in TILES:
                        self.change[:, at] = middle(at)
                    return carry

                lax.fori_loop(2, 2 << level, again, 0)
                for at in TILES:
                    last(at, self.base[:, at], self.change[:, at])

        else:
            for at in TILES:
                self.base[:, at], self.change[:, at] = first(at)

            @pl.when(level == 0)
            def _():
                for at in TILES:
                    last(at, self.base[:, at], middle(at))

            @pl.when(level > 0)
            def _():
                def pair(_, carry):
                    for at in TILES:
                        change, left = self.next_turn(solver, at, self.base[:, at], middle(at))
                        self.change[:, at] = change
                        finish(at, change, left)
                    return carry

                lax.fori_loop(0, (1 << level) + (1 << level) // 2, pair, 0)

    def fine_steps(self, solver, field, middle, level):
        def first(at, change, _):
            middle[:, at] = field[:, at] + change

        def second(at, change, _):
            field[:, at] = middle[:, at] + change

        def step(_, carry):
            self.solve(solver, field, None, level, first)
            self.solve(solver, middle, field, level, second)
            return carry

        lax.fori_loop(0, FACTOR, step, 0)


def main_kernel(
    where, own, beside, across, corner, fine, coarse, fine_mode, coarse_mode,
    spread, saturation,
    half, rest, mine, delta, source, balance, counts,
    field, middle, keep, base, change, errors, squares, fine_balance,
):
    interval, strip = where[0], where[1]
    width = own.shape[1]
    pieces = (own, beside, across, corner)

    def place(k):
        return pl.ds(pl.multiple_of(jnp.bitwise_xor(strip, k) * width, COLS), width)

    for k, piece in enumerate(pieces):
        decay = piece[S : 2 * S, :]
        delta[:, place(k)] = CENTRE - decay
        source[:, place(k)] = piece[2 * S : 3 * S, :]
        for mode, shift, total in ((fine_mode, 1.0, fine_balance), (coarse_mode, 1.0 / FACTOR, balance)):
            losses = (shift + 4.0 * spread[...] + decay) * mode[...]
            total[:, place(k)] = 1.0 / jnp.sum(losses, axis=0, keepdims=True)
    grid = Grid(delta, source, spread, saturation, base, change)
    fine_solver = Solver(fine, fine_mode, fine_balance, 1.0, 2, False)
    coarse_solver = Solver(coarse, coarse_mode, balance, 1.0 / FACTOR, 3, True)

    def keep_own(condition):
        @pl.when(condition)
        def _():
            mine[...] = field[:, pl.ds(pl.multiple_of(strip * width, COLS), width)]

    def attempt(state):
        level = state[0]
        counts[0] = level
        for k, piece in enumerate(pieces):
            field[:, place(k)] = piece[0:S, :]
        keep_own(interval == 0)

        def interval_steps(phase, carry):
            for at in TILES:
                keep[:, at] = field[:, at]
            grid.fine_steps(fine_solver, field, middle, level)
            keep_own(interval == phase + 1)
            return carry

        lax.fori_loop(0, 2, interval_steps, 0)

        def defect(at, moved, left):
            here = field[:, at]
            middle[:, at] = here - keep[:, at] - moved
            errors[:, at] = left * left
            squares[:, at] = here * here

        grid.solve(coarse_solver, keep, None, level, defect)
        return level + 1, jnp.sum(errors[...]) <= (ENOUGH * ENOUGH) * jnp.sum(squares[...])

    lax.while_loop(lambda state: jnp.logical_not(state[1]) & (state[0] < 6), attempt, (jnp.int32(0), False))
    level = counts[0]

    @pl.when(interval <= 3)
    def _():
        for at in TILES:
            field[:, at] = keep[:, at]

    for at in TILES:
        keep[:, at] = middle[:, at]

    def linked(at, moved, _):
        middle[:, at] = field[:, at] + moved + keep[:, at]

    def link(_, carry):
        grid.solve(coarse_solver, field, None, level, linked)
        for at in TILES:
            field[:, at] = middle[:, at]
        return carry

    lax.fori_loop(4, interval, link, 0)

    def interval_steps(_, carry):
        for at in TILES:
            keep[:, at] = field[:, at]
        grid.fine_steps(fine_solver, field, middle, level)
        return carry

    lax.fori_loop(0, 2, interval_steps, 0)

    def handed(at, moved, _):
        middle[:, at] = field[:, at] - jnp.where(interval <= 4, 0.0, keep[:, at] + moved)

    grid.solve(coarse_solver, keep, None, level, handed)
    keep_own((interval == 3) | (interval == 4))
    half[...] = middle[:, half_at(strip, 0)]
    rest[...] = middle[:, half_at(strip, 1)]


def half_at(strip, other):
    core = jnp.bitwise_xor(jnp.bitwise_and(strip, 1), other)
    return pl.ds(pl.multiple_of(core * (CELLS // 2), COLS), CELLS // 2)


def whole():
    return jax.ShapeDtypeStruct((S, CELLS), jnp.float32)


def half_grid():
    return jax.ShapeDtypeStruct((S, CELLS // 2), jnp.float32)


def line():
    return jax.ShapeDtypeStruct((1, CELLS), jnp.float32)


def scratch(count):
    return [pltpu.VMEM((S, CELLS), jnp.float32) for _ in range(count)]


def run_main(where, pieces, *shared):
    width = pieces[0].shape[1]
    return pl.pallas_call(
        main_kernel,
        out_shape=[
            half_grid(), half_grid(), jax.ShapeDtypeStruct((S, width), jnp.float32),
            whole(), whole(), line(), jax.ShapeDtypeStruct((1,), jnp.int32),
        ],
        in_specs=[SMEM] + [VMEM] * 10,
        out_specs=[VMEM] * 6 + [SMEM],
        scratch_shapes=scratch(7) + [pltpu.VMEM((1, CELLS), jnp.float32)],
        compiler_params=PARAMS,
        name="to_payload",
    )(where, *pieces, *shared)


def slot_of(member, core, j):
    near = jnp.bitwise_xor(member, jnp.where(core == 0, (0, 1, 3, 2)[j % 4], (0, 3, 1, 2)[j % 4]))
    return jnp.bitwise_xor(near, j // 4 * 4)


def chain_kernel(length, sources, *refs):
    where, counts = refs[:2]
    arrived, refs = refs[2 : 2 + 2 * sources], refs[2 + 2 * sources :]
    payloads, rest = refs[: 2 * length], refs[2 * length :]
    seeded = sources == 0
    coefficients = rest[:2]
    coarse, mode, balance, spread, saturation = rest[2:7]
    half, mine, field, middle, base, change, delta, source, stage, fetched, passed = rest[7:]
    member, strip = where[0] % length, where[1]
    width = mine.shape[1]

    def held(piece, slot, k):
        return pltpu.make_async_copy(piece, stage.at[slot, :, half_at(strip, k)], passed.at[slot, k])

    def coming(k):
        return pltpu.make_async_copy(arrived[k], field.at[:, half_at(strip, k % 2)], fetched.at[k % 2])

    if sources > 1:
        for way in range(sources):

            @pl.when(member // 4 == way)
            def _():
                for k in range(2):
                    coming(2 * way + k).start()

    elif sources > 0:
        for k in range(2):
            coming(k).start()
    copies = [
        pltpu.make_async_copy(source_ref, target, fetched.at[2 + k])
        for k, (source_ref, target) in enumerate(zip(coefficients, (delta, source)))
    ]
    for copy in copies:
        copy.start()
    for j in range(length):
        for k in range(2):
            core = jnp.bitwise_xor(jnp.bitwise_and(strip, 1), k)
            held(payloads[2 * j + k], slot_of(member, core, j), k).start()
    for copy in copies + ([] if seeded else [coming(0), coming(1)]):
        copy.wait()
    grid = Grid(delta, source, spread, saturation, base, change)
    solver = Solver(coarse, mode, balance, 1.0 / FACTOR, 3, True)

    def show(slot, state):
        @pl.when(member == slot)
        def _():
            mine[...] = state[:, pl.ds(pl.multiple_of(strip * width, COLS), width)]

    def fetched_payload(slot):
        for k in range(2):
            held(payloads[k], slot, k).wait()

    def link(slot, carry):
        fetched_payload(slot)

        def linked(at, moved, _):
            middle[:, at] = field[:, at] + moved + stage[slot, :, at]

        grid.solve(solver, field, None, counts[0], linked)
        for at in TILES:
            field[:, at] = middle[:, at]
        show(slot, field)
        return carry

    if seeded:
        fetched_payload(0)
        field[...] = stage[0]
        show(0, field)
    lax.fori_loop(1 if seeded else 0, length, link, 0)
    half[...] = field[:, half_at(strip, 0)]


def run_chain(where, counts, arrived, payloads, coefficients, shared):
    length, sources = len(payloads) // 2, len(arrived) // 2
    return pl.pallas_call(
        functools.partial(chain_kernel, length, sources),
        out_shape=[half_grid(), jax.ShapeDtypeStruct((S, CELLS // 4), jnp.float32)],
        in_specs=[SMEM, SMEM] + [ANY] * (2 * sources + 2 * length + 2) + [VMEM] * 5,
        out_specs=[VMEM, VMEM],
        scratch_shapes=scratch(6)
        + [
            pltpu.VMEM((length, S, CELLS), jnp.float32),
            pltpu.SemaphoreType.DMA((4,)),
            pltpu.SemaphoreType.DMA((length, 2)),
        ],
        compiler_params=PARAMS,
        name=f"links_{length}_{sources}",
    )(where, counts, *arrived, *payloads, *coefficients, *shared)


def neighbour_route():
    route = []
    for tm in range(32):
        for strip in range(4):
            high, low, core = (tm // 4) % 2, strip // 2, strip % 2
            y = high * 2 + low
            from_y = (y + 1) % 4 if core else (y - 1) % 4
            from_tm = tm + ((from_y // 2) - high) * 4
            route.append((from_tm * 4 + (from_y % 2) * 2 + core, tm * 4 + strip))
    return route


def per_device(initial_field, decay_rates, source, diffusion, saturation, conversion):
    strip, interval = lax.axis_index("space"), lax.axis_index("tm")
    where = jnp.stack([interval, strip]).astype(jnp.int32)
    own = jnp.concatenate([initial_field, decay_rates, source], axis=0)
    swap = [(0, 1), (1, 0), (2, 3), (3, 2)]
    across = lax.ppermute(own, ("tm", "space"), neighbour_route())
    beside = lax.ppermute(own, "space", swap)
    corner = lax.ppermute(across, "space", swap)

    off_diagonal = conversion * (1.0 - jnp.eye(S, dtype=jnp.float32))
    outflow = jnp.sum(off_diagonal, axis=0)
    still = 4.0 * diffusion + outflow
    centre = jnp.eye(S, dtype=jnp.float32) * (still + CENTRE)[:, None] - off_diagonal
    fine, coarse, fine_mode, coarse_mode = invert_pair(
        centre + jnp.eye(S, dtype=jnp.float32), centre + jnp.eye(S, dtype=jnp.float32) / FACTOR
    )
    fine, coarse = wide(fine), wide(coarse)
    spread, saturation = diffusion[:, None], saturation[:, None]
    half, rest, mine, *coefficients, balance, counts = run_main(
        where, (own, beside, across, corner), fine, coarse, fine_mode, coarse_mode, spread, saturation
    )
    shared = (coarse, coarse_mode, balance, spread, saturation)
    def swapped(piece):
        return [piece, lax.ppermute(piece, "space", swap)]

    def exchanged(piece, flips, lowest):
        route = [(4 * (i ^ flips[c % 2]) + c, 4 * i + c) for i in range(lowest, 32) for c in range(4)]
        return lax.ppermute(piece, ("tm", "space"), route)

    def doubled(piece, lowest):
        second = exchanged(piece, (1, 3), lowest)
        return [second, exchanged(piece, (3, 1), lowest), exchanged(second, (3, 1), lowest)]

    near = sum([swapped(piece) for piece in doubled(half, 4)], [half, rest])

    def advance(active, arrived, payloads, last, mine):
        def run():
            return tuple(run_chain(where, counts, arrived, payloads, coefficients, shared))

        return lax.cond(active, run, lambda: (last, mine))

    def hop(last, start, distance, length):
        return lax.ppermute(last, "tm", [(start - distance + m, start + m) for m in range(length)])

    last, mine = advance(interval // 4 == 1, [], near, half, mine)
    behind, last = lax.optimization_barrier((half, last))
    partner = swapped(lax.ppermute(behind, "tm", [(i ^ 4, i) for i in range(16, 32)]))
    payloads = near + partner + sum([swapped(piece) for piece in doubled(partner[0], 16)], [])
    for quarter in (2, 3):
        arrived = swapped(hop(last, 4 * quarter, 4, 4))
        last, mine = advance(interval // 4 == quarter, arrived, near, last, mine)
    arrived = swapped(hop(last, 16, 4, 4)) + swapped(hop(last, 20, 8, 4))
    last, mine = advance(interval // 8 == 2, arrived, payloads, last, mine)
    arrived = hop(last, 24, 8, 8)
    last, mine = advance(interval // 8 == 3, swapped(arrived), payloads, last, mine)
    return mine[None]


def solution(mesh):
    in_specs = (P(None, "space"), P(None, "space"), P(None, "space"), P(), P(), P())
    out_specs = P("tm", None, "space")
    return jax.shard_map(
        per_device, mesh=mesh, in_specs=in_specs, out_specs=out_specs, check_vma=False
    )
```

```python
import functools

import jax
import jax.numpy as jnp
from jax import lax
from jax.experimental import pallas as pl
from jax.experimental.pallas import tpu as pltpu
from jax.sharding import PartitionSpec as P

COLS = 128
FACTOR = 4
NEWTON = 2
ROWS = 16
CELLS = 2048
S = 48
TILE = 256
CENTRE = 0.4
ENOUGH = 2.2e-3

VMEM = pl.BlockSpec(memory_space=pltpu.VMEM)
ANY = pl.BlockSpec(memory_space=pl.ANY)
TILES = [slice(start, start + TILE) for start in range(0, CELLS, TILE)]
SMEM = pl.BlockSpec(memory_space=pltpu.SMEM)
PARAMS = pltpu.CompilerParams(vmem_limit_bytes=48 << 20)


def halves(value):
    high = value.astype(jnp.bfloat16)
    low = (value - high.astype(jnp.float32)).astype(jnp.bfloat16)
    return high, low


def stacked(value):
    high, low = halves(value)
    return jnp.concatenate([high, low, high], axis=0)


def wide(matrix):
    rounded = lax.reduce_precision(matrix, 8, 7)
    high, low = rounded.astype(jnp.bfloat16), (matrix - rounded).astype(jnp.bfloat16)
    return jnp.concatenate([high, high, low], axis=1)


def times(matrix, value):
    return jnp.dot(matrix, stacked(value), preferred_element_type=jnp.float32)


def invert_kernel(matrix_ref, out_ref, first_mode, second_mode):
    lane = lax.broadcasted_iota(jnp.int32, (S, COLS), 1)
    row_number = lax.broadcasted_iota(jnp.int32, (S, COLS), 0)
    lane_row = lax.broadcasted_iota(jnp.int32, (1, COLS), 1)
    out_ref[...] = matrix_ref[...]

    def taken(values, numbers, number):
        return jnp.sum(jnp.where(numbers == number, values, 0.0), axis=1, keepdims=True)

    def both(numbers, first, second):
        return jnp.where(numbers < 64, first, second)

    def eliminate(turn, _):
        k = 2 * turn
        current = out_ref[...]
        rows = [out_ref[pl.ds(k + p, 1), :] for p in range(2)]
        columns = [
            both(lane, taken(current, lane, k + p), taken(current, lane, k + 64 + p)) for p in range(2)
        ]
        block = [
            [both(lane_row, taken(row, lane_row, k + p), taken(row, lane_row, k + 64 + p)) for p in range(2)]
            for row in rows
        ]
        scale = 1.0 / (block[0][0] * block[1][1] - block[0][1] * block[1][0])
        at = [(lane_row == k + p) | (lane_row == k + 64 + p) for p in range(2)]
        either = at[0] | at[1]
        freed = [jnp.where(either, jnp.where(at[p], 1.0, 0.0), rows[p]) for p in range(2)]
        scaled = [
            scale * (block[1][1] * freed[0] - block[0][1] * freed[1]),
            scale * (block[0][0] * freed[1] - block[1][0] * freed[0]),
        ]
        updated = jnp.where(either, 0.0, current) - columns[0] * scaled[0] - columns[1] * scaled[1]
        for p in range(2):
            updated = jnp.where(row_number == k + p, scaled[p], updated)
        out_ref[...] = updated
        return 0

    lax.fori_loop(0, S // 2, eliminate, 0)
    for at, mode in ((0, first_mode), (64, second_mode)):
        power = out_ref[:, at : at + S]
        for _ in range(2):
            power = jnp.dot(power, power, precision=lax.Precision.HIGHEST, preferred_element_type=jnp.float32)
        mode[...] = jnp.sum(power, axis=1, keepdims=True)


def invert_pair(first, second):
    gap = jnp.zeros((S, 16), jnp.float32)
    pair = jnp.concatenate([first, gap, second, gap], axis=1)
    pair = pair + jnp.where(jnp.arange(COLS) % 64 >= S, 1.0, 0.0)[None, :]
    column = jax.ShapeDtypeStruct((S, 1), jnp.float32)
    inverted, first_mode, second_mode = pl.pallas_call(
        invert_kernel,
        out_shape=[jax.ShapeDtypeStruct((S, COLS), jnp.float32), column, column],
        in_specs=[VMEM],
        out_specs=[VMEM] * 3,
        name="invert_pair",
    )(pair)
    return inverted[:, :S], inverted[:, 64 : 64 + S], first_mode, second_mode


class Solver:
    def __init__(self, inverse, mode, balance, shift, turns, early):
        self.inverse, self.balance, self.shift = inverse, balance, shift
        self.turns, self.early = turns, early
        self.mode = jnp.broadcast_to(mode[...], (S, TILE))


class Grid:
    def __init__(self, delta, source, spread, saturation, base, change):
        self.delta, self.source = delta, source
        self.spread = jnp.broadcast_to(spread[...], (S, COLS))
        self.saturation = jnp.broadcast_to(saturation[...], (S, COLS))
        self.base, self.change = base, change
        lane = lax.broadcasted_iota(jnp.int32, (S, COLS), 1)
        self.not_first, self.not_last = lane != 0, lane != COLS - 1

    def driven(self, field, r):
        at = slice(r * COLS, (r + 1) * COLS)
        here = field[:, at]
        around = jnp.where(self.not_first, pltpu.roll(here, 1, 1), 0.0) + jnp.where(
            self.not_last, pltpu.roll(here, COLS - 1, 1), 0.0
        )
        if r > 0:
            around = around + field[:, (r - 1) * COLS : r * COLS]
        if r < ROWS - 1:
            around = around + field[:, (r + 1) * COLS : (r + 2) * COLS]
        saturated = self.saturation * (here / (1.0 + here * here) - here)
        return self.spread * around + self.delta[:, at] * here + saturated + self.source[:, at]

    def share(self, solver, at, left):
        return solver.mode * (jnp.sum(left, axis=0, keepdims=True) * solver.balance[:, at])

    def first_turn(self, solver, field, previous, at):
        r = at.start // COLS
        here = field[:, at]
        value = jnp.concatenate([self.driven(field, r + k) for k in range(2)], axis=1)
        value = value + (solver.shift * here if previous is None else previous[:, at])
        base = times(solver.inverse[...], value) - here
        if solver.early:
            return base, base + self.share(solver, at, self.delta[:, at] * base)
        return base, base

    def next_turn(self, solver, at, base, before):
        change = base + times(solver.inverse[...], self.delta[:, at] * before)
        left = self.delta[:, at] * (change - before)
        return change + self.share(solver, at, left), left

    def solve(self, solver, field, previous, level, finish):
        def first(at):
            return self.first_turn(solver, field, previous, at)

        def last(at, base, change):
            finish(at, *self.next_turn(solver, at, base, change))

        def middle(at):
            return self.next_turn(solver, at, self.base[:, at], self.change[:, at])[0]

        if solver.turns == 2:

            @pl.when(level == 0)
            def _():
                for at in TILES:
                    last(at, *first(at))

            @pl.when(level > 0)
            def _():
                for at in TILES:
                    self.base[:, at], self.change[:, at] = first(at)

                def again(_, carry):
                    for at in TILES:
                        self.change[:, at] = middle(at)
                    return carry

                lax.fori_loop(2, 2 << level, again, 0)
                for at in TILES:
                    last(at, self.base[:, at], self.change[:, at])

        else:
            for at in TILES:
                self.base[:, at], self.change[:, at] = first(at)

            @pl.when(level == 0)
            def _():
                for at in TILES:
                    last(at, self.base[:, at], middle(at))

            @pl.when(level > 0)
            def _():
                def pair(_, carry):
                    for at in TILES:
                        change, left = self.next_turn(solver, at, self.base[:, at], middle(at))
                        self.change[:, at] = change
                        finish(at, change, left)
                    return carry

                lax.fori_loop(0, (1 << level) + (1 << level) // 2, pair, 0)

    def fine_steps(self, solver, field, middle, level):
        def first(at, change, _):
            middle[:, at] = field[:, at] + change

        def second(at, change, _):
            field[:, at] = middle[:, at] + change

        def step(_, carry):
            self.solve(solver, field, None, level, first)
            self.solve(solver, middle, field, level, second)
            return carry

        lax.fori_loop(0, FACTOR, step, 0)


def main_kernel(
    where, own, beside, across, corner, fine, coarse, fine_mode, coarse_mode,
    spread, saturation,
    half, rest, mine, delta, source, balance, counts,
    field, middle, keep, base, change, errors, squares, fine_balance,
):
    interval, strip = where[0], where[1]
    width = own.shape[1]
    pieces = (own, beside, across, corner)

    def place(k):
        return pl.ds(pl.multiple_of(jnp.bitwise_xor(strip, k) * width, COLS), width)

    for k, piece in enumerate(pieces):
        decay = piece[S : 2 * S, :]
        delta[:, place(k)] = CENTRE - decay
        source[:, place(k)] = piece[2 * S : 3 * S, :]
        for mode, shift, total in ((fine_mode, 1.0, fine_balance), (coarse_mode, 1.0 / FACTOR, balance)):
            losses = (shift + 4.0 * spread[...] + decay) * mode[...]
            total[:, place(k)] = 1.0 / jnp.sum(losses, axis=0, keepdims=True)
    grid = Grid(delta, source, spread, saturation, base, change)
    fine_solver = Solver(fine, fine_mode, fine_balance, 1.0, 2, False)
    coarse_solver = Solver(coarse, coarse_mode, balance, 1.0 / FACTOR, 2, True)

    def keep_own(condition):
        @pl.when(condition)
        def _():
            mine[...] = field[:, pl.ds(pl.multiple_of(strip * width, COLS), width)]

    def attempt(state):
        level = state[0]
        counts[0] = level
        for k, piece in enumerate(pieces):
            field[:, place(k)] = piece[0:S, :]
        keep_own(interval == 0)

        def interval_steps(phase, carry):
            for at in TILES:
                keep[:, at] = field[:, at]
            grid.fine_steps(fine_solver, field, middle, level)
            keep_own(interval == phase + 1)
            return carry

        lax.fori_loop(0, 2, interval_steps, 0)

        def defect(at, moved, left):
            here = field[:, at]
            middle[:, at] = here - keep[:, at] - moved
            errors[:, at] = left * left
            squares[:, at] = here * here

        grid.solve(coarse_solver, keep, None, level, defect)
        return level + 1, jnp.sum(errors[...]) <= (ENOUGH * ENOUGH) * jnp.sum(squares[...])

    lax.while_loop(lambda state: jnp.logical_not(state[1]) & (state[0] < 6), attempt, (jnp.int32(0), False))
    level = counts[0]

    @pl.when(interval <= 3)
    def _():
        for at in TILES:
            field[:, at] = keep[:, at]

    for at in TILES:
        keep[:, at] = middle[:, at]

    def linked(at, moved, _):
        middle[:, at] = field[:, at] + moved + keep[:, at]

    def link(_, carry):
        grid.solve(coarse_solver, field, None, level, linked)
        for at in TILES:
            field[:, at] = middle[:, at]
        return carry

    lax.fori_loop(4, interval, link, 0)

    def interval_steps(_, carry):
        for at in TILES:
            keep[:, at] = field[:, at]
        grid.fine_steps(fine_solver, field, middle, level)
        return carry

    lax.fori_loop(0, 2, interval_steps, 0)

    def handed(at, moved, _):
        middle[:, at] = field[:, at] - jnp.where(interval <= 4, 0.0, keep[:, at] + moved)

    grid.solve(coarse_solver, keep, None, level, handed)
    keep_own((interval == 3) | (interval == 4))
    half[...] = middle[:, half_at(strip, 0)]
    rest[...] = middle[:, half_at(strip, 1)]


def half_at(strip, other):
    core = jnp.bitwise_xor(jnp.bitwise_and(strip, 1), other)
    return pl.ds(pl.multiple_of(core * (CELLS // 2), COLS), CELLS // 2)


def whole():
    return jax.ShapeDtypeStruct((S, CELLS), jnp.float32)


def half_grid():
    return jax.ShapeDtypeStruct((S, CELLS // 2), jnp.float32)


def line():
    return jax.ShapeDtypeStruct((1, CELLS), jnp.float32)


def scratch(count):
    return [pltpu.VMEM((S, CELLS), jnp.float32) for _ in range(count)]


def run_main(where, pieces, *shared):
    width = pieces[0].shape[1]
    return pl.pallas_call(
        main_kernel,
        out_shape=[
            half_grid(), half_grid(), jax.ShapeDtypeStruct((S, width), jnp.float32),
            whole(), whole(), line(), jax.ShapeDtypeStruct((1,), jnp.int32),
        ],
        in_specs=[SMEM] + [VMEM] * 10,
        out_specs=[VMEM] * 6 + [SMEM],
        scratch_shapes=scratch(7) + [pltpu.VMEM((1, CELLS), jnp.float32)],
        compiler_params=PARAMS,
        name="to_payload",
    )(where, *pieces, *shared)


def slot_of(member, core, j):
    near = jnp.bitwise_xor(member, jnp.where(core == 0, (0, 1, 3, 2)[j % 4], (0, 3, 1, 2)[j % 4]))
    return jnp.bitwise_xor(near, j // 4 * 4)


def chain_kernel(length, sources, *refs):
    where, counts = refs[:2]
    arrived, refs = refs[2 : 2 + 2 * sources], refs[2 + 2 * sources :]
    payloads, rest = refs[: 2 * length], refs[2 * length :]
    seeded = sources == 0
    coefficients = rest[:2]
    coarse, mode, balance, spread, saturation = rest[2:7]
    half, mine, field, middle, base, change, delta, source, stage, fetched, passed = rest[7:]
    member, strip = where[0] % length, where[1]
    width = mine.shape[1]

    def held(piece, slot, k):
        return pltpu.make_async_copy(piece, stage.at[slot, :, half_at(strip, k)], passed.at[slot, k])

    def coming(k):
        return pltpu.make_async_copy(arrived[k], field.at[:, half_at(strip, k % 2)], fetched.at[k % 2])

    if sources > 1:
        for way in range(sources):

            @pl.when(member // 4 == way)
            def _():
                for k in range(2):
                    coming(2 * way + k).start()

    elif sources > 0:
        for k in range(2):
            coming(k).start()
    copies = [
        pltpu.make_async_copy(source_ref, target, fetched.at[2 + k])
        for k, (source_ref, target) in enumerate(zip(coefficients, (delta, source)))
    ]
    for copy in copies:
        copy.start()
    for j in range(length):
        for k in range(2):
            core = jnp.bitwise_xor(jnp.bitwise_and(strip, 1), k)
            held(payloads[2 * j + k], slot_of(member, core, j), k).start()
    for copy in copies + ([] if seeded else [coming(0), coming(1)]):
        copy.wait()
    grid = Grid(delta, source, spread, saturation, base, change)
    solver = Solver(coarse, mode, balance, 1.0 / FACTOR, 2, True)

    def show(slot, state):
        @pl.when(member == slot)
        def _():
            mine[...] = state[:, pl.ds(pl.multiple_of(strip * width, COLS), width)]

    def fetched_payload(slot):
        for k in range(2):
            held(payloads[k], slot, k).wait()

    def link(slot, carry):
        fetched_payload(slot)

        def linked(at, moved, _):
            middle[:, at] = field[:, at] + moved + stage[slot, :, at]

        grid.solve(solver, field, None, counts[0], linked)
        for at in TILES:
            field[:, at] = middle[:, at]
        show(slot, field)
        return carry

    if seeded:
        fetched_payload(0)
        field[...] = stage[0]
        show(0, field)
    lax.fori_loop(1 if seeded else 0, length, link, 0)
    half[...] = field[:, half_at(strip, 0)]


def run_chain(where, counts, arrived, payloads, coefficients, shared):
    length, sources = len(payloads) // 2, len(arrived) // 2
    return pl.pallas_call(
        functools.partial(chain_kernel, length, sources),
        out_shape=[half_grid(), jax.ShapeDtypeStruct((S, CELLS // 4), jnp.float32)],
        in_specs=[SMEM, SMEM] + [ANY] * (2 * sources + 2 * length + 2) + [VMEM] * 5,
        out_specs=[VMEM, VMEM],
        scratch_shapes=scratch(6)
        + [
            pltpu.VMEM((length, S, CELLS), jnp.float32),
            pltpu.SemaphoreType.DMA((4,)),
            pltpu.SemaphoreType.DMA((length, 2)),
        ],
        compiler_params=PARAMS,
        name=f"links_{length}_{sources}",
    )(where, counts, *arrived, *payloads, *coefficients, *shared)


def neighbour_route():
    route = []
    for tm in range(32):
        for strip in range(4):
            high, low, core = (tm // 4) % 2, strip // 2, strip % 2
            y = high * 2 + low
            from_y = (y + 1) % 4 if core else (y - 1) % 4
            from_tm = tm + ((from_y // 2) - high) * 4
            route.append((from_tm * 4 + (from_y % 2) * 2 + core, tm * 4 + strip))
    return route


def per_device(initial_field, decay_rates, source, diffusion, saturation, conversion):
    strip, interval = lax.axis_index("space"), lax.axis_index("tm")
    where = jnp.stack([interval, strip]).astype(jnp.int32)
    own = jnp.concatenate([initial_field, decay_rates, source], axis=0)
    swap = [(0, 1), (1, 0), (2, 3), (3, 2)]
    across = lax.ppermute(own, ("tm", "space"), neighbour_route())
    beside = lax.ppermute(own, "space", swap)
    corner = lax.ppermute(across, "space", swap)

    off_diagonal = conversion * (1.0 - jnp.eye(S, dtype=jnp.float32))
    outflow = jnp.sum(off_diagonal, axis=0)
    still = 4.0 * diffusion + outflow
    centre = jnp.eye(S, dtype=jnp.float32) * (still + CENTRE)[:, None] - off_diagonal
    fine, coarse, fine_mode, coarse_mode = invert_pair(
        centre + jnp.eye(S, dtype=jnp.float32), centre + jnp.eye(S, dtype=jnp.float32) / FACTOR
    )
    fine, coarse = wide(fine), wide(coarse)
    spread, saturation = diffusion[:, None], saturation[:, None]
    half, rest, mine, *coefficients, balance, counts = run_main(
        where, (own, beside, across, corner), fine, coarse, fine_mode, coarse_mode, spread, saturation
    )
    shared = (coarse, coarse_mode, balance, spread, saturation)
    def swapped(piece):
        return [piece, lax.ppermute(piece, "space", swap)]

    def exchanged(piece, flips, lowest):
        route = [(4 * (i ^ flips[c % 2]) + c, 4 * i + c) for i in range(lowest, 32) for c in range(4)]
        return lax.ppermute(piece, ("tm", "space"), route)

    def doubled(piece, lowest):
        second = exchanged(piece, (1, 3), lowest)
        return [second, exchanged(piece, (3, 1), lowest), exchanged(second, (3, 1), lowest)]

    near = sum([swapped(piece) for piece in doubled(half, 4)], [half, rest])

    def advance(active, arrived, payloads, last, mine):
        def run():
            return tuple(run_chain(where, counts, arrived, payloads, coefficients, shared))

        return lax.cond(active, run, lambda: (last, mine))

    def hop(last, start, distance, length):
        return lax.ppermute(last, "tm", [(start - distance + m, start + m) for m in range(length)])

    last, mine = advance(interval // 4 == 1, [], near, half, mine)
    behind, last = lax.optimization_barrier((half, last))
    partner = swapped(lax.ppermute(behind, "tm", [(i ^ 4, i) for i in range(16, 32)]))
    payloads = near + partner + sum([swapped(piece) for piece in doubled(partner[0], 16)], [])
    for quarter in (2, 3):
        arrived = swapped(hop(last, 4 * quarter, 4, 4))
        last, mine = advance(interval // 4 == quarter, arrived, near, last, mine)
    arrived = swapped(hop(last, 16, 4, 4)) + swapped(hop(last, 20, 8, 4))
    last, mine = advance(interval // 8 == 2, arrived, payloads, last, mine)
    arrived = hop(last, 24, 8, 8)
    last, mine = advance(interval // 8 == 3, swapped(arrived), payloads, last, mine)
    return mine[None]


def solution(mesh):
    in_specs = (P(None, "space"), P(None, "space"), P(None, "space"), P(), P(), P())
    out_specs = P("tm", None, "space")
    return jax.shard_map(
        per_device, mesh=mesh, in_specs=in_specs, out_specs=out_specs, check_vma=False
    )
```

```python
import functools

import jax
import jax.numpy as jnp
from jax import lax
from jax.experimental import pallas as pl
from jax.experimental.pallas import tpu as pltpu
from jax.sharding import PartitionSpec as P

COLS = 128
FACTOR = 4
NEWTON = 2
ROWS = 16
CELLS = 2048
S = 48
TILE = 256
CENTRE = 0.4
ENOUGH = 2.2e-3

VMEM = pl.BlockSpec(memory_space=pltpu.VMEM)
ANY = pl.BlockSpec(memory_space=pl.ANY)
TILES = [slice(start, start + TILE) for start in range(0, CELLS, TILE)]
SMEM = pl.BlockSpec(memory_space=pltpu.SMEM)
PARAMS = pltpu.CompilerParams(vmem_limit_bytes=48 << 20)


def halves(value):
    high = value.astype(jnp.bfloat16)
    low = (value - high.astype(jnp.float32)).astype(jnp.bfloat16)
    return high, low


def stacked(value):
    high, low = halves(value)
    return jnp.concatenate([high, low, high], axis=0)


def wide(matrix):
    rounded = lax.reduce_precision(matrix, 8, 7)
    high, low = rounded.astype(jnp.bfloat16), (matrix - rounded).astype(jnp.bfloat16)
    return jnp.concatenate([high, high, low], axis=1)


def times(matrix, value):
    return jnp.dot(matrix, stacked(value), preferred_element_type=jnp.float32)


def invert_kernel(matrix_ref, out_ref, first_mode, second_mode):
    lane = lax.broadcasted_iota(jnp.int32, (S, COLS), 1)
    row_number = lax.broadcasted_iota(jnp.int32, (S, COLS), 0)
    lane_row = lax.broadcasted_iota(jnp.int32, (1, COLS), 1)
    out_ref[...] = matrix_ref[...]

    def taken(values, numbers, number):
        return jnp.sum(jnp.where(numbers == number, values, 0.0), axis=1, keepdims=True)

    def both(numbers, first, second):
        return jnp.where(numbers < 64, first, second)

    def eliminate(turn, _):
        k = 2 * turn
        current = out_ref[...]
        rows = [out_ref[pl.ds(k + p, 1), :] for p in range(2)]
        columns = [
            both(lane, taken(current, lane, k + p), taken(current, lane, k + 64 + p)) for p in range(2)
        ]
        block = [
            [both(lane_row, taken(row, lane_row, k + p), taken(row, lane_row, k + 64 + p)) for p in range(2)]
            for row in rows
        ]
        scale = 1.0 / (block[0][0] * block[1][1] - block[0][1] * block[1][0])
        at = [(lane_row == k + p) | (lane_row == k + 64 + p) for p in range(2)]
        either = at[0] | at[1]
        freed = [jnp.where(either, jnp.where(at[p], 1.0, 0.0), rows[p]) for p in range(2)]
        scaled = [
            scale * (block[1][1] * freed[0] - block[0][1] * freed[1]),
            scale * (block[0][0] * freed[1] - block[1][0] * freed[0]),
        ]
        updated = jnp.where(either, 0.0, current) - columns[0] * scaled[0] - columns[1] * scaled[1]
        for p in range(2):
            updated = jnp.where(row_number == k + p, scaled[p], updated)
        out_ref[...] = updated
        return 0

    lax.fori_loop(0, S // 2, eliminate, 0)
    for at, mode in ((0, first_mode), (64, second_mode)):
        power = out_ref[:, at : at + S]
        for _ in range(2):
            power = jnp.dot(power, power, precision=lax.Precision.HIGHEST, preferred_element_type=jnp.float32)
        mode[...] = jnp.sum(power, axis=1, keepdims=True)


def invert_pair(first, second):
    gap = jnp.zeros((S, 16), jnp.float32)
    pair = jnp.concatenate([first, gap, second, gap], axis=1)
    pair = pair + jnp.where(jnp.arange(COLS) % 64 >= S, 1.0, 0.0)[None, :]
    column = jax.ShapeDtypeStruct((S, 1), jnp.float32)
    inverted, first_mode, second_mode = pl.pallas_call(
        invert_kernel,
        out_shape=[jax.ShapeDtypeStruct((S, COLS), jnp.float32), column, column],
        in_specs=[VMEM],
        out_specs=[VMEM] * 3,
        name="invert_pair",
    )(pair)
    return inverted[:, :S], inverted[:, 64 : 64 + S], first_mode, second_mode


class Solver:
    def __init__(self, inverse, mode, balance, shift, turns, early):
        self.inverse, self.balance, self.shift = inverse, balance, shift
        self.turns, self.early = turns, early
        self.mode = jnp.broadcast_to(mode[...], (S, TILE))


class Grid:
    def __init__(self, delta, source, spread, saturation, base, change):
        self.delta, self.source = delta, source
        self.spread = jnp.broadcast_to(spread[...], (S, COLS))
        self.saturation = jnp.broadcast_to(saturation[...], (S, COLS))
        self.base, self.change = base, change
        lane = lax.broadcasted_iota(jnp.int32, (S, COLS), 1)
        self.not_first, self.not_last = lane != 0, lane != COLS - 1

    def driven(self, field, r):
        at = slice(r * COLS, (r + 1) * COLS)
        here = field[:, at]
        around = jnp.where(self.not_first, pltpu.roll(here, 1, 1), 0.0) + jnp.where(
            self.not_last, pltpu.roll(here, COLS - 1, 1), 0.0
        )
        if r > 0:
            around = around + field[:, (r - 1) * COLS : r * COLS]
        if r < ROWS - 1:
            around = around + field[:, (r + 1) * COLS : (r + 2) * COLS]
        saturated = self.saturation * (here / (1.0 + here * here) - here)
        return self.spread * around + self.delta[:, at] * here + saturated + self.source[:, at]

    def share(self, solver, at, left):
        return solver.mode * (jnp.sum(left, axis=0, keepdims=True) * solver.balance[:, at])

    def first_turn(self, solver, field, previous, at):
        r = at.start // COLS
        here = field[:, at]
        value = jnp.concatenate([self.driven(field, r + k) for k in range(2)], axis=1)
        value = value + (solver.shift * here if previous is None else previous[:, at])
        base = times(solver.inverse[...], value) - here
        if solver.early:
            return base, base + self.share(solver, at, self.delta[:, at] * base)
        return base, base

    def next_turn(self, solver, at, base, before):
        change = base + times(solver.inverse[...], self.delta[:, at] * before)
        left = self.delta[:, at] * (change - before)
        return change + self.share(solver, at, left), left

    def solve(self, solver, field, previous, level, finish):
        def first(at):
            return self.first_turn(solver, field, previous, at)

        def last(at, base, change):
            finish(at, *self.next_turn(solver, at, base, change))

        def middle(at):
            return self.next_turn(solver, at, self.base[:, at], self.change[:, at])[0]

        if solver.turns == 2:

            @pl.when(level == 0)
            def _():
                for at in TILES:
                    last(at, *first(at))

            @pl.when(level > 0)
            def _():
                for at in TILES:
                    self.base[:, at], self.change[:, at] = first(at)

                def again(_, carry):
                    for at in TILES:
                        self.change[:, at] = middle(at)
                    return carry

                lax.fori_loop(2, 2 << level, again, 0)
                for at in TILES:
                    last(at, self.base[:, at], self.change[:, at])

        else:
            for at in TILES:
                self.base[:, at], self.change[:, at] = first(at)

            @pl.when(level == 0)
            def _():
                for at in TILES:
                    last(at, self.base[:, at], middle(at))

            @pl.when(level > 0)
            def _():
                def pair(_, carry):
                    for at in TILES:
                        change, left = self.next_turn(solver, at, self.base[:, at], middle(at))
                        self.change[:, at] = change
                        finish(at, change, left)
                    return carry

                lax.fori_loop(0, (1 << level) + (1 << level) // 2, pair, 0)

    def fine_steps(self, solver, field, middle, level):
        def first(at, change, _):
            middle[:, at] = field[:, at] + change

        def second(at, change, _):
            field[:, at] = middle[:, at] + change

        def step(_, carry):
            self.solve(solver, field, None, level, first)
            self.solve(solver, middle, field, level, second)
            return carry

        lax.fori_loop(0, FACTOR, step, 0)


def main_kernel(
    where, own, beside, across, corner, fine, coarse, fine_mode, coarse_mode,
    spread, saturation,
    half, rest, mine, delta, source, balance, counts,
    field, middle, keep, base, change, errors, squares, fine_balance,
):
    interval, strip = where[0], where[1]
    width = own.shape[1]
    pieces = (own, beside, across, corner)

    def place(k):
        return pl.ds(pl.multiple_of(jnp.bitwise_xor(strip, k) * width, COLS), width)

    for k, piece in enumerate(pieces):
        decay = piece[S : 2 * S, :]
        delta[:, place(k)] = CENTRE - decay
        source[:, place(k)] = piece[2 * S : 3 * S, :]
        for mode, shift, total in ((fine_mode, 1.0, fine_balance), (coarse_mode, 1.0 / FACTOR, balance)):
            losses = (shift + 4.0 * spread[...] + decay) * mode[...]
            total[:, place(k)] = 1.0 / jnp.sum(losses, axis=0, keepdims=True)
    grid = Grid(delta, source, spread, saturation, base, change)
    fine_solver = Solver(fine, fine_mode, fine_balance, 1.0, 2, False)
    coarse_solver = Solver(coarse, coarse_mode, balance, 1.0 / FACTOR, 2, True)

    def keep_own(condition):
        @pl.when(condition)
        def _():
            mine[...] = field[:, pl.ds(pl.multiple_of(strip * width, COLS), width)]

    def attempt(state):
        level = state[0]
        counts[0] = level
        for k, piece in enumerate(pieces):
            field[:, place(k)] = piece[0:S, :]
        keep_own(interval == 0)

        def interval_steps(phase, carry):
            for at in TILES:
                keep[:, at] = field[:, at]
            grid.fine_steps(fine_solver, field, middle, level)
            keep_own(interval == phase + 1)
            return carry

        lax.fori_loop(0, 2, interval_steps, 0)

        def defect(at, moved, left):
            here = field[:, at]
            middle[:, at] = here - keep[:, at] - moved
            errors[:, at] = left * left
            squares[:, at] = here * here

        grid.solve(coarse_solver, keep, None, level, defect)
        return level + 1, jnp.sum(errors[...]) <= (ENOUGH * ENOUGH) * jnp.sum(squares[...])

    lax.while_loop(lambda state: jnp.logical_not(state[1]) & (state[0] < 6), attempt, (jnp.int32(0), False))
    level = counts[0]

    @pl.when(interval <= 3)
    def _():
        for at in TILES:
            field[:, at] = keep[:, at]

    for at in TILES:
        keep[:, at] = middle[:, at]

    def linked(at, moved, _):
        middle[:, at] = field[:, at] + moved + keep[:, at]

    def link(_, carry):
        grid.solve(coarse_solver, field, None, level, linked)
        for at in TILES:
            field[:, at] = middle[:, at]
        return carry

    lax.fori_loop(4, interval, link, 0)

    def interval_steps(_, carry):
        for at in TILES:
            keep[:, at] = field[:, at]
        grid.fine_steps(fine_solver, field, middle, level)
        return carry

    lax.fori_loop(0, 2, interval_steps, 0)

    def handed(at, moved, _):
        middle[:, at] = field[:, at] - jnp.where(interval <= 4, 0.0, keep[:, at] + moved)

    grid.solve(coarse_solver, keep, None, level, handed)
    keep_own((interval == 3) | (interval == 4))
    half[...] = middle[:, half_at(strip, 0)]
    rest[...] = middle[:, half_at(strip, 1)]


def half_at(strip, other):
    core = jnp.bitwise_xor(jnp.bitwise_and(strip, 1), other)
    return pl.ds(pl.multiple_of(core * (CELLS // 2), COLS), CELLS // 2)


def whole():
    return jax.ShapeDtypeStruct((S, CELLS), jnp.float32)


def half_grid():
    return jax.ShapeDtypeStruct((S, CELLS // 2), jnp.float32)


def line():
    return jax.ShapeDtypeStruct((1, CELLS), jnp.float32)


def scratch(count):
    return [pltpu.VMEM((S, CELLS), jnp.float32) for _ in range(count)]


def run_main(where, pieces, *shared):
    width = pieces[0].shape[1]
    return pl.pallas_call(
        main_kernel,
        out_shape=[
            half_grid(), half_grid(), jax.ShapeDtypeStruct((S, width), jnp.float32),
            whole(), whole(), line(), jax.ShapeDtypeStruct((1,), jnp.int32),
        ],
        in_specs=[SMEM] + [VMEM] * 10,
        out_specs=[VMEM] * 6 + [SMEM],
        scratch_shapes=scratch(7) + [pltpu.VMEM((1, CELLS), jnp.float32)],
        compiler_params=PARAMS,
        name="to_payload",
    )(where, *pieces, *shared)


def slot_of(member, core, j):
    near = jnp.bitwise_xor(member, jnp.where(core == 0, (0, 1, 3, 2)[j % 4], (0, 3, 1, 2)[j % 4]))
    return jnp.bitwise_xor(near, j // 4 * 4)


def chain_kernel(length, sources, *refs):
    where, counts = refs[:2]
    arrived, refs = refs[2 : 2 + 2 * sources], refs[2 + 2 * sources :]
    payloads, rest = refs[: 2 * length], refs[2 * length :]
    seeded = sources == 0
    coefficients = rest[:2]
    coarse, mode, balance, spread, saturation = rest[2:7]
    half, mine, field, middle, base, change, delta, source, stage, fetched, passed = rest[7:]
    member, strip = where[0] % length, where[1]
    width = mine.shape[1]

    def held(piece, slot, k):
        return pltpu.make_async_copy(piece, stage.at[slot, :, half_at(strip, k)], passed.at[slot, k])

    def coming(k):
        return pltpu.make_async_copy(arrived[k], field.at[:, half_at(strip, k % 2)], fetched.at[k % 2])

    if sources > 1:
        for way in range(sources):

            @pl.when(member // 4 == way)
            def _():
                for k in range(2):
                    coming(2 * way + k).start()

    elif sources > 0:
        for k in range(2):
            coming(k).start()
    copies = [
        pltpu.make_async_copy(source_ref, target, fetched.at[2 + k])
        for k, (source_ref, target) in enumerate(zip(coefficients, (delta, source)))
    ]
    for copy in copies:
        copy.start()
    for j in range(length):
        for k in range(2):
            core = jnp.bitwise_xor(jnp.bitwise_and(strip, 1), k)
            held(payloads[2 * j + k], slot_of(member, core, j), k).start()
    for copy in copies + ([] if seeded else [coming(0), coming(1)]):
        copy.wait()
    grid = Grid(delta, source, spread, saturation, base, change)
    solver = Solver(coarse, mode, balance, 1.0 / FACTOR, 2, True)

    def show(slot, state):
        @pl.when(member == slot)
        def _():
            mine[...] = state[:, pl.ds(pl.multiple_of(strip * width, COLS), width)]

    def fetched_payload(slot):
        for k in range(2):
            held(payloads[k], slot, k).wait()

    def link(slot, before, after):
        fetched_payload(slot)

        def linked(at, moved, _):
            after[:, at] = before[:, at] + moved + stage[slot, :, at]

        grid.solve(solver, before, None, counts[0], linked)
        show(slot, after)

    def two_links(pair, carry):
        link(2 * pair, field, middle)
        link(2 * pair + 1, middle, field)
        return carry

    if seeded:
        fetched_payload(0)
        middle[...] = stage[0]
        show(0, middle)
        link(1, middle, field)
    lax.fori_loop(1 if seeded else 0, length // 2, two_links, 0)
    half[...] = field[:, half_at(strip, 0)]


def run_chain(where, counts, arrived, payloads, coefficients, shared):
    length, sources = len(payloads) // 2, len(arrived) // 2
    return pl.pallas_call(
        functools.partial(chain_kernel, length, sources),
        out_shape=[half_grid(), jax.ShapeDtypeStruct((S, CELLS // 4), jnp.float32)],
        in_specs=[SMEM, SMEM] + [ANY] * (2 * sources + 2 * length + 2) + [VMEM] * 5,
        out_specs=[VMEM, VMEM],
        scratch_shapes=scratch(6)
        + [
            pltpu.VMEM((length, S, CELLS), jnp.float32),
            pltpu.SemaphoreType.DMA((4,)),
            pltpu.SemaphoreType.DMA((length, 2)),
        ],
        compiler_params=PARAMS,
        name=f"links_{length}_{sources}",
    )(where, counts, *arrived, *payloads, *coefficients, *shared)


def neighbour_route():
    route = []
    for tm in range(32):
        for strip in range(4):
            high, low, core = (tm // 4) % 2, strip // 2, strip % 2
            y = high * 2 + low
            from_y = (y + 1) % 4 if core else (y - 1) % 4
            from_tm = tm + ((from_y // 2) - high) * 4
            route.append((from_tm * 4 + (from_y % 2) * 2 + core, tm * 4 + strip))
    return route


def per_device(initial_field, decay_rates, source, diffusion, saturation, conversion):
    strip, interval = lax.axis_index("space"), lax.axis_index("tm")
    where = jnp.stack([interval, strip]).astype(jnp.int32)
    own = jnp.concatenate([initial_field, decay_rates, source], axis=0)
    swap = [(0, 1), (1, 0), (2, 3), (3, 2)]
    across = lax.ppermute(own, ("tm", "space"), neighbour_route())
    beside = lax.ppermute(own, "space", swap)
    corner = lax.ppermute(across, "space", swap)

    off_diagonal = conversion * (1.0 - jnp.eye(S, dtype=jnp.float32))
    outflow = jnp.sum(off_diagonal, axis=0)
    still = 4.0 * diffusion + outflow
    centre = jnp.eye(S, dtype=jnp.float32) * (still + CENTRE)[:, None] - off_diagonal
    fine, coarse, fine_mode, coarse_mode = invert_pair(
        centre + jnp.eye(S, dtype=jnp.float32), centre + jnp.eye(S, dtype=jnp.float32) / FACTOR
    )
    fine, coarse = wide(fine), wide(coarse)
    spread, saturation = diffusion[:, None], saturation[:, None]
    half, rest, mine, *coefficients, balance, counts = run_main(
        where, (own, beside, across, corner), fine, coarse, fine_mode, coarse_mode, spread, saturation
    )
    shared = (coarse, coarse_mode, balance, spread, saturation)
    def swapped(piece):
        return [piece, lax.ppermute(piece, "space", swap)]

    def exchanged(piece, flips, lowest):
        route = [(4 * (i ^ flips[c % 2]) + c, 4 * i + c) for i in range(lowest, 32) for c in range(4)]
        return lax.ppermute(piece, ("tm", "space"), route)

    def doubled(piece, lowest):
        second = exchanged(piece, (1, 3), lowest)
        return [second, exchanged(piece, (3, 1), lowest), exchanged(second, (3, 1), lowest)]

    near = sum([swapped(piece) for piece in doubled(half, 4)], [half, rest])

    def advance(active, arrived, payloads, last, mine):
        def run():
            return tuple(run_chain(where, counts, arrived, payloads, coefficients, shared))

        return lax.cond(active, run, lambda: (last, mine))

    def hop(last, start, distance, length):
        return lax.ppermute(last, "tm", [(start - distance + m, start + m) for m in range(length)])

    last, mine = advance(interval // 4 == 1, [], near, half, mine)
    behind, last = lax.optimization_barrier((half, last))
    partner = swapped(lax.ppermute(behind, "tm", [(i ^ 4, i) for i in range(16, 32)]))
    payloads = near + partner + sum([swapped(piece) for piece in doubled(partner[0], 16)], [])
    for quarter in (2, 3):
        arrived = swapped(hop(last, 4 * quarter, 4, 4))
        last, mine = advance(interval // 4 == quarter, arrived, near, last, mine)
    arrived = swapped(hop(last, 16, 4, 4)) + swapped(hop(last, 20, 8, 4))
    last, mine = advance(interval // 8 == 2, arrived, payloads, last, mine)
    arrived = hop(last, 24, 8, 8)
    last, mine = advance(interval // 8 == 3, swapped(arrived), payloads, last, mine)
    return mine[None]


def solution(mesh):
    in_specs = (P(None, "space"), P(None, "space"), P(None, "space"), P(), P(), P())
    out_specs = P("tm", None, "space")
    return jax.shard_map(
        per_device, mesh=mesh, in_specs=in_specs, out_specs=out_specs, check_vma=False
    )
```
